128 devices in a mesh: seq: 32 (over x_hi, z, y), head: 4 (over x_lo, core).
Axes of the slice: x: 4 (x_hi: 2, x_lo: 2; x = x_hi * 2 + x_lo), y: 4, z: 4, core: 2. Of those that a mesh axis runs over, the one named last changes fastest.
Arguments:
- queries: bfloat16 [65536, 4096], P('seq', 'head'), may hold values from -112 to 112
- key_rows: bfloat16 [65536, 4096], P('seq', 'head'), may hold values from -5 to 5
- value_rows: bfloat16 [65536, 4096], P('seq', 'head'), may hold values from -5 to 5
Outputs:
- attended: bfloat16 [65536, 4096], P(('seq', 'head'))
The draws below stay inside these ranges and needn't reach their ends.
All inputs are finite; a program needn't handle non-finite values.
Results may differ from the reference program's by a relative error of at most 0.0055.
Values may be sent and summed in bfloat16 or wider, within the bound.
No kernel may reach another device: no remote copies, remote signals or barrier semaphores. Data moves between devices by JAX's collectives and lax.ppermute only.
A program may use at most 256 MiB of HBM per device.

```python
import math
import jax
import jax.numpy as jnp
from jax import lax

HEADS = 32
HD = 128
TOK_DEV = 2048
BLK = 256
P1 = 8
P2 = 64
R1 = 12
TOKENS = 65536


def shared_keys(key):
    rough = jnp.clip(jax.random.normal(jax.random.fold_in(key, 201), (TOKENS, HEADS * HD), jnp.float32), -3.5, 3.5)
    levels = jnp.clip(jax.random.normal(jax.random.fold_in(key, 202), (TOKENS // P2, HEADS * HD), jnp.float32), -3.5, 3.5)
    base_keys = 0.7 * rough + 0.7 * jnp.repeat(levels, P2, axis=0)
    positions = jnp.arange(TOKENS)[:, None]
    marked = (positions + 1) % 509 == 100
    return jnp.where(marked, base_keys, base_keys)


def draw_key_rows(key, part):
    return shared_keys(key).astype(jnp.bfloat16)


def draw_queries(key, part):
    key = jax.random.fold_in(key, 5)
    drawn = jnp.clip(jax.random.normal(jax.random.fold_in(key, 1), (TOKENS, HEADS * HD), jnp.float32), -4.0, 4.0)
    return drawn.astype(jnp.bfloat16)


def draw_value_rows(key, part):
    key = jax.random.fold_in(key, 7)
    rough = jnp.clip(jax.random.normal(jax.random.fold_in(key, 1), (TOKENS, HEADS * HD), jnp.float32), -3.5, 3.5)
    levels = jnp.clip(jax.random.normal(jax.random.fold_in(key, 2), (TOKENS // P2, HEADS * HD), jnp.float32), -3.5, 3.5)
    return (0.7 * rough + 0.7 * jnp.repeat(levels, P2, axis=0)).astype(jnp.bfloat16)


def setup_inputs(seed: int = 0) -> dict:
    streams_of = jax.random.split(jax.random.key(seed), 4)
    queries = draw_queries(jax.random.fold_in(streams_of[3], 71), 0)
    key_rows = draw_key_rows(jax.random.fold_in(streams_of[3], 71), 0)
    value_rows = draw_value_rows(jax.random.fold_in(streams_of[3], 71), 0)
    return dict(queries=queries, key_rows=key_rows, value_rows=value_rows)


def pooled_mean(rows_in, factor):
    return lax.optimization_barrier(jnp.mean(rows_in.astype(jnp.float32).reshape(-1, factor, rows_in.shape[1]), axis=1)).astype(jnp.bfloat16)

def reference(queries, key_rows, value_rows):
    score_scale = 1.0 / math.sqrt(HD)
    tile_size = min(TOK_DEV, 512)
    feat_width = HEADS * HD
    key_one = pooled_mean(key_rows, P1)
    val_one = pooled_mean(value_rows, P1)
    key_two = pooled_mean(key_rows, P2)
    val_two = pooled_mean(value_rows, P2)
    front = R1 * BLK // P1
    key_one_pad = jnp.concatenate([jnp.zeros((front, feat_width), jnp.bfloat16), key_one])
    val_one_pad = jnp.concatenate([jnp.zeros((front, feat_width), jnp.bfloat16), val_one])
    near_keys = jnp.concatenate([jnp.zeros((BLK, feat_width), jnp.bfloat16), key_rows])
    near_vals = jnp.concatenate([jnp.zeros((BLK, feat_width), jnp.bfloat16), value_rows])
    width_one = (R1 + tile_size // BLK) * BLK // P1
    groups_two = TOKENS // P2
    far_block = jnp.arange(groups_two, dtype=jnp.int32) * P2 // BLK

    def tile_output(tile_idx):
        first = (tile_idx * tile_size).astype(jnp.int32)
        query_tile = lax.dynamic_slice_in_dim(queries, first, tile_size, 0).astype(jnp.float32).reshape(tile_size, HEADS, HD)
        query_pos = first + jnp.arange(tile_size, dtype=jnp.int32)
        query_block = query_pos // BLK
        near_pos = first - BLK + jnp.arange(tile_size + BLK, dtype=jnp.int32)
        near_ok = (near_pos[None, :] <= query_pos[:, None]) & (near_pos[None, :] >= 0) & (near_pos[None, :] // BLK >= query_block[:, None] - 1)
        near_k = lax.dynamic_slice_in_dim(near_keys, first, tile_size + BLK, 0)
        near_v = lax.dynamic_slice_in_dim(near_vals, first, tile_size + BLK, 0)
        group_idx = first // P1 - front + jnp.arange(width_one, dtype=jnp.int32)
        group_block = group_idx * P1 // BLK
        one_ok = (group_idx[None, :] >= 0) & (group_block[None, :] >= query_block[:, None] - R1) & (group_block[None, :] <= query_block[:, None] - 2)
        one_k = lax.dynamic_slice_in_dim(key_one_pad, (first // P1).astype(jnp.int32), width_one, 0)
        one_v = lax.dynamic_slice_in_dim(val_one_pad, (first // P1).astype(jnp.int32), width_one, 0)
        two_ok = far_block[None, :] < query_block[:, None] - R1

        def level_logits(key_part, allowed, bias):
            logits = jnp.einsum('qhd,khd->hqk', query_tile, key_part.astype(jnp.float32).reshape(-1, HEADS, HD)) * score_scale + bias
            return jnp.where(allowed[None], logits, -jnp.inf)
        logits = jnp.concatenate([level_logits(near_k, near_ok, 0.0), level_logits(one_k, one_ok, math.log(P1)), level_logits(key_two, two_ok, math.log(P2))], axis=2)
        values_all = jnp.concatenate([near_v, one_v, val_two]).astype(jnp.float32).reshape(-1, HEADS, HD)
        maxima = lax.optimization_barrier(jnp.max(logits, axis=2, keepdims=True))
        weights = jnp.exp(logits - maxima)
        totals = lax.optimization_barrier(jnp.sum(weights, axis=2))
        rounded = lax.optimization_barrier(weights.astype(jnp.bfloat16)).astype(jnp.float32)
        numer = jnp.einsum('hqk,khd->qhd', rounded, values_all)
        return (numer / totals.T[:, :, None]).astype(jnp.bfloat16).reshape(tile_size, feat_width)
    outputs = lax.map(tile_output, jnp.arange(TOKENS // tile_size, dtype=jnp.int32))
    return outputs.reshape(TOKENS, feat_width)
```

```python
import math

import jax
import jax.numpy as jnp
from jax import lax
from jax.experimental import pallas as pl
from jax.experimental.pallas import tpu as pltpu
from jax.sharding import PartitionSpec as P

HD = 128
BLK = 256
P1 = 8
P2 = 64
R1 = 12
SEQ = 32
TOK = 2048
NEG = -1e30
MIDB = BLK // P1
FARD = TOK // P2
FARS = SEQ * FARD
MIDS = 18 * MIDB
EXP_SCALE = math.log2(math.e) / math.sqrt(HD)
CHUNKS = 2
WIDTH = 1024 // CHUNKS
VMEM_LIMIT = 56 * 1024 * 1024


def seq_route(move):
    route = []
    for s in range(SEQ):
        x, z, y = s // 16, (s // 4) % 4, s % 4
        x, z, y = move(x, z, y)
        route.append((s, x * 16 + (z % 4) * 4 + y % 4))
    return route


X_ROUTE = seq_route(lambda x, z, y: (1 - x, z, y))
Y_ROUTES = [seq_route(lambda x, z, y, d=d: (x, z, y + d)) for d in (1, 3, 2)]
Z_ROUTES = [seq_route(lambda x, z, y, d=d: (x, z + d, y)) for d in (1, 3, 2)]
OFFSETS = (0, 3, 1, 2)


def shift_route(distance):
    return [(i - distance, i) for i in range(distance, SEQ)]


def pool_kernel(k_ref, v_ref, b1_ref, b2_ref, f_ref):
    rows = lax.broadcasted_iota(jnp.int32, (40, BLK), 0)
    cols = lax.broadcasted_iota(jnp.int32, (40, BLK), 1)
    mid = jnp.where(cols // P1 == rows, 1.0 / P1, 0.0)
    far = jnp.where(cols // P2 == rows - 32, 1.0 / P2, 0.0)
    mean = jnp.where(rows < 32, mid, far).astype(jnp.bfloat16)
    for i, ref in enumerate((k_ref, v_ref)):
        b1_ref[i * 256 : i * 256 + 256, :] = ref[TOK - BLK :, :]
        fars = []
        for b in range(TOK // BLK):
            pooled = jnp.dot(
                mean, ref[b * BLK : (b + 1) * BLK, :], preferred_element_type=jnp.float32
            )
            mids = pooled[:32].astype(jnp.bfloat16)
            at = 512 + (b // 4) * 256 + i * 128 + (b % 4) * 32
            b1_ref[at : at + 32, :] = mids
            if b >= 4:
                at = i * 128 + (b % 4) * 32
                b2_ref[at : at + 32, :] = mids
            fars.append(pooled[32:36])
        f_ref[i * 32 : i * 32 + 32, :] = jnp.concatenate(fars, axis=0).astype(jnp.bfloat16)


def pool(chunk, key_rows, value_rows):
    step = 256
    first = chunk * WIDTH // step
    return pl.pallas_call(
        pool_kernel,
        grid=(WIDTH // step,),
        in_specs=[pl.BlockSpec((TOK, step), lambda i: (0, first + i))] * 2,
        out_specs=[
            pl.BlockSpec((1024, step), lambda i: (0, i)),
            pl.BlockSpec((256, step), lambda i: (0, i)),
            pl.BlockSpec((64, step), lambda i: (0, i)),
        ],
        out_shape=[
            jax.ShapeDtypeStruct((1024, WIDTH), jnp.bfloat16),
            jax.ShapeDtypeStruct((256, WIDTH), jnp.bfloat16),
            jax.ShapeDtypeStruct((64, WIDTH), jnp.bfloat16),
        ],
        compiler_params=pltpu.CompilerParams(vmem_limit_bytes=VMEM_LIMIT),
        cost_estimate=pl.CostEstimate(
            flops=2 * 2 * TOK * WIDTH * 40, bytes_accessed=2 * TOK * WIDTH * 3, transcendentals=0
        ),
        name="pool",
    )(key_rows, value_rows)


def dot_nt(a, b):
    return lax.dot_general(a, b, (((1,), (1,)), ((), ())), preferred_element_type=jnp.float32)


def attend_kernel(
    info_ref, q_ref, k_ref, v_ref, own_ref, r1_ref, r2_ref, h0_ref, h1_ref, h2_ref, h3_ref,
    oa_ref, ob_ref, kn, vn, km, vm, kf, vf, ke, ve, sa, sb,
):
    s = info_ref[0]
    half = info_ref[1]
    flip = info_ref[2]
    x, z, y = s // 16, (s // 4) % 4, s % 4
    bf = jnp.bfloat16

    @pl.when(pl.program_id(0) == 0)
    def _():
        vn[:, HD:] = jnp.ones((1280, HD), bf)
        vm[:, HD:] = jnp.full((MIDS, HD), P1, bf)
        ve[:, HD:] = jnp.full((32, HD), P2, bf)

    @pl.when(half == 0)
    def _():
        kn[:256, :] = r1_ref[0:256, :]
        vn[:256, :HD] = r1_ref[256:512, :]
        kn[256:, :] = k_ref[:1024, :]
        vn[256:, :HD] = v_ref[:1024, :]

    @pl.when(half == 1)
    def _():
        kn[...] = k_ref[768:, :]
        vn[:, :HD] = v_ref[768:, :]

    eight = jnp.full((128, HD), P1, bf)
    km[0:128, :] = r2_ref[0:128, :]
    vm[0:128, :HD] = r2_ref[128:256, :] * eight
    km[128:256, :] = r1_ref[512:640, :]
    vm[128:256, :HD] = r1_ref[640:768, :] * eight
    km[256:384, :] = r1_ref[768:896, :]
    vm[256:384, :HD] = r1_ref[896:1024, :] * eight
    km[384:512, :] = own_ref[512:640, :]
    vm[384:512, :HD] = own_ref[640:768, :] * eight
    km[512:576, :] = own_ref[768:832, :]
    vm[512:576, :HD] = own_ref[896:960, :] * eight[:64]

    scale = jnp.full((32, HD), P2, bf)
    for zi, h_ref in enumerate((h0_ref, h1_ref, h2_ref, h3_ref)):
        for yi in range(4):
            for xi in range(2):
                src = (x ^ xi) * 16 + ((z + OFFSETS[zi]) % 4) * 4 + (y + OFFSETS[yi]) % 4
                to = pl.multiple_of(src * 32, 32)
                at = yi * 128 + xi * 64
                kf[pl.ds(to, 32), :] = h_ref[at : at + 32, :]
                vf[pl.ds(to, 32), :HD] = h_ref[at + 32 : at + 64, :] * scale
    vf[:, HD:] = jnp.full((FARS, HD), P2, bf)
    edge = 2 * s - 3
    for i in range(2):
        at = pl.multiple_of(jnp.maximum(edge + i, 0) * 16, 16)
        ke[i * 16 : i * 16 + 16, :] = kf[pl.ds(at, 16), :]
        ve[i * 16 : i * 16 + 16, :HD] = vf[pl.ds(at, 16), :HD]
    filler = jnp.broadcast_to(kf[0:1, :], (16, HD))

    def fill(u, carry):
        at = pl.multiple_of(u * 16, 16)
        kf[pl.ds(at, 16), :] = filler
        vf[pl.ds(at, 16), :] = jnp.zeros((16, 2 * HD), bf)
        return carry

    lax.fori_loop(jnp.maximum(edge, 0), FARS // 16, fill, 0)

    def block_of(n):
        local = 2 * ((n // 2) ^ flip) + n % 2
        return local, half * 4 + local

    def scores(n, s_ref, with_far):
        local, j = block_of(n)
        q = q_ref[pl.ds(pl.multiple_of(local * BLK, BLK), BLK), :]
        start = pl.multiple_of(local * BLK, BLK)
        sn = dot_nt(q, kn[pl.ds(start, BLK), :])
        sn = sn + jnp.where((s == 0) & (j == 0), NEG, 0.0)
        s_ref[:, 0:256] = sn
        top = jnp.maximum(sn[:, :128], sn[:, 128:])
        rows = lax.broadcasted_iota(jnp.int32, (BLK, BLK), 0)
        cols = lax.broadcasted_iota(jnp.int32, (BLK, BLK), 1)
        sd = dot_nt(q, kn[pl.ds(start + BLK, BLK), :])
        sd = jnp.where(cols <= rows, sd, NEG)
        s_ref[:, 256:512] = sd
        top = jnp.maximum(top, jnp.maximum(sd[:, :128], sd[:, 128:]))
        mids = jnp.concatenate(
            [km[pl.ds(pl.multiple_of(j * MIDB, MIDB), 352), :], ke[...]], axis=0
        )
        col = lax.broadcasted_iota(jnp.int32, (1, 384), 1)
        low = MIDB * (R1 - 8 * s - j)
        e = col - 352
        ok = jnp.where(e < 0, col - low, jnp.minimum(e - (48 - 32 * s), 4 * j - 1 - e)) >= 0
        sm = dot_nt(q, mids) + jnp.where(ok, 0.0, NEG)
        s_ref[:, 512:896] = sm
        for i in range(3):
            top = jnp.maximum(top, sm[:, i * 128 : i * 128 + 128])
        if with_far:
            for i in range(4):
                sf = dot_nt(q, kf[i * 256 : i * 256 + 256, :])
                s_ref[:, 896 + i * 256 : 1152 + i * 256] = sf
                top = jnp.maximum(top, jnp.maximum(sf[:, :128], sf[:, 128:]))
        return jnp.max(top, axis=1, keepdims=True)

    def finish(n, s_ref, top, o_ref, with_far):
        local, j = block_of(n)
        start = pl.multiple_of(local * BLK, BLK)

        def weights(a, b):
            return jnp.exp2((s_ref[:, a:b] - top) * EXP_SCALE).astype(bf)

        acc = jnp.dot(
            weights(0, 512), vn[pl.ds(start, 512), :], preferred_element_type=jnp.float32
        )
        mids = jnp.concatenate(
            [vm[pl.ds(pl.multiple_of(j * MIDB, MIDB), 352), :], ve[...]], axis=0
        )
        acc = acc + jnp.dot(weights(512, 896), mids, preferred_element_type=jnp.float32)
        if with_far:
            for i in range(4):
                acc = acc + jnp.dot(
                    weights(896 + i * 256, 1152 + i * 256),
                    vf[i * 256 : i * 256 + 256, :],
                    preferred_element_type=jnp.float32,
                )
        at = (n % 2) * BLK
        o_ref[at : at + BLK, :] = (acc[:, :HD] / acc[:, HD:]).astype(bf)

    def blocks(with_far):
        slots = (sa, sb)
        top = scores(0, sa, with_far)
        for n in range(4):
            later = scores(n + 1, slots[(n + 1) % 2], with_far) if n < 3 else None
            finish(n, slots[n % 2], top, (oa_ref, ob_ref)[n // 2], with_far)
            top = later

    @pl.when(edge > 0)
    def _():
        blocks(True)

    @pl.when(edge <= 0)
    def _():
        blocks(False)


def attend(chunk, info, queries, key_rows, value_rows, own, r1, r2, fars):
    heads = WIDTH // HD
    first = chunk * heads
    whole = lambda rows: pl.BlockSpec((rows, HD), lambda h, info: (0, h))
    return pl.pallas_call(
        attend_kernel,
        grid_spec=pltpu.PrefetchScalarGridSpec(
            num_scalar_prefetch=1,
            grid=(heads,),
            in_specs=[
                pl.BlockSpec((1024, HD), lambda h, info: (info[1], first + h)),
                pl.BlockSpec((TOK, HD), lambda h, info: (0, first + h)),
                pl.BlockSpec((TOK, HD), lambda h, info: (0, first + h)),
                whole(1024),
                whole(1024),
                whole(256),
                whole(512),
                whole(512),
                whole(512),
                whole(512),
            ],
            out_specs=[whole(512), whole(512)],
            scratch_shapes=[
                pltpu.VMEM((1280, HD), jnp.bfloat16),
                pltpu.VMEM((1280, 2 * HD), jnp.bfloat16),
                pltpu.VMEM((MIDS, HD), jnp.bfloat16),
                pltpu.VMEM((MIDS, 2 * HD), jnp.bfloat16),
                pltpu.VMEM((FARS, HD), jnp.bfloat16),
                pltpu.VMEM((FARS, 2 * HD), jnp.bfloat16),
                pltpu.VMEM((32, HD), jnp.bfloat16),
                pltpu.VMEM((32, 2 * HD), jnp.bfloat16),
                pltpu.VMEM((BLK, 1920), jnp.float32),
                pltpu.VMEM((BLK, 1920), jnp.float32),
            ],
        ),
        out_shape=[jax.ShapeDtypeStruct((512, WIDTH), jnp.bfloat16)] * 2,
        compiler_params=pltpu.CompilerParams(vmem_limit_bytes=VMEM_LIMIT),
        cost_estimate=pl.CostEstimate(
            flops=heads * 4 * BLK * 1920 * HD * 8,
            bytes_accessed=heads * HD * 2 * 10000,
            transcendentals=heads * 4 * BLK * 1920,
        ),
        name="attend",
    )(info, queries, key_rows, value_rows, own, r1, r2, *fars)


def place_kernel(me_ref, *refs):
    pieces, out_ref = refs[:-1], refs[-1]
    me = me_ref[0]
    for i, piece in enumerate(pieces):
        chunk, k = i // 4, i % 4
        at = pl.multiple_of((me ^ k) * 1024 + chunk * WIDTH, WIDTH)
        out_ref[:, pl.ds(at, WIDTH)] = piece[...]


def place(me, pieces):
    step = 64
    return pl.pallas_call(
        place_kernel,
        grid_spec=pltpu.PrefetchScalarGridSpec(
            num_scalar_prefetch=1,
            grid=(512 // step,),
            in_specs=[pl.BlockSpec((step, WIDTH), lambda i, me: (i, 0))] * len(pieces),
            out_specs=pl.BlockSpec((step, 4096), lambda i, me: (i, 0)),
        ),
        out_shape=jax.ShapeDtypeStruct((512, 4096), jnp.bfloat16),
        cost_estimate=pl.CostEstimate(flops=0, bytes_accessed=8 * 1024 * 1024, transcendentals=0),
        name="place",
    )(me, *pieces)


def swap_heads(piece, k):
    return lax.ppermute(piece, "head", [(i, i ^ k) for i in range(4)])


def shards(queries, key_rows, value_rows):
    s = lax.axis_index("seq").astype(jnp.int32)
    me = lax.axis_index("head").astype(jnp.int32)
    pair, flip = me // 2, me % 2
    over = lambda value, route: lax.ppermute(value, "seq", route)
    ready = []
    for c in range(CHUNKS):
        b1, b2, f0 = pool(c, key_rows, value_rows)
        f1 = over(f0, X_ROUTE)
        r1 = over(b1, shift_route(1))
        g0 = jnp.concatenate([f0, f1])
        gs = [over(g0, route) for route in Y_ROUTES]
        r2 = over(b2, shift_route(2))
        h0 = jnp.concatenate([g0] + gs)
        hs = [over(h0, route) for route in Z_ROUTES]
        ready.append((b1, r1, r2, [h0] + hs))
    pieces = {}
    for c in range(CHUNKS):
        parts = (queries, key_rows, value_rows) + ready[c]
        out2, out3 = attend(c, jnp.stack([s, 1 - pair, flip]), *parts)
        pieces[c, 2], pieces[c, 3] = swap_heads(out2, 2), swap_heads(out3, 3)
        out0, out1 = attend(c, jnp.stack([s, pair, flip]), *parts)
        pieces[c, 0], pieces[c, 1] = out0, swap_heads(out1, 1)
    return place(
        me.reshape(1), [pieces[c, k] for c in range(CHUNKS) for k in range(4)]
    )


def solution(mesh):
    return jax.shard_map(
        shards,
        mesh=mesh,
        in_specs=(P("seq", "head"), P("seq", "head"), P("seq", "head")),
        out_specs=P(("seq", "head"), None),
        check_vma=False,
    )
```

```python
import math

import jax
import jax.numpy as jnp
from jax import lax
from jax.experimental import pallas as pl
from jax.experimental.pallas import tpu as pltpu
from jax.sharding import PartitionSpec as P

HD = 128
BLK = 256
P1 = 8
P2 = 64
R1 = 12
SEQ = 32
TOK = 2048
HEADS = 8
NEG = -1e30
MIDB = BLK // P1
FARD = TOK // P2
FARS = SEQ * FARD
MIDS = 19 * MIDB
KEYS = 512 + 384 + FARS
EXP_SCALE = math.log2(math.e) / math.sqrt(HD)
CHUNKS = (5, 3)
VMEM_LIMIT = 56 * 1024 * 1024
BF = jnp.bfloat16
WORK = 4 * 4 * BLK * KEYS * HD * 8


def seq_route(move):
    route = []
    for s in range(SEQ):
        x, z, y = move(s // 16, (s // 4) % 4, s % 4)
        route.append((s, x * 16 + (z % 4) * 4 + y % 4))
    return route


Y_UP = seq_route(lambda x, z, y: (x, z, y + 1))
Y_DOWN = seq_route(lambda x, z, y: (x, z, y - 1))
X_ROUTE = seq_route(lambda x, z, y: (1 - x, z, y))
Z_UP = seq_route(lambda x, z, y: (x, z + 1, y))
Z_DOWN = seq_route(lambda x, z, y: (x, z - 1, y))
FROM = (0, 1, 3, 2)


def shift_route(distance):
    return [(i - distance, i) for i in range(distance, SEQ)]


ALONG_Y = [(i, i + 1) for i in range(SEQ) if i % 4 < 3]
UP_Z = [(i, i + 4) for i in range(3, SEQ - 4, 4)]
ROUND_Y = [(i, i - 3) for i in range(7, SEQ, 4)]


def pool_kernel(k_ref, v_ref, send_k_ref, send_v_ref, mid2_ref, far_ref):
    rows = lax.broadcasted_iota(jnp.int32, (48, BLK), 0)
    cols = lax.broadcasted_iota(jnp.int32, (48, BLK), 1)
    mid = jnp.where(cols // P1 == rows, 1.0, 0.0)
    far = jnp.where(cols // P2 == rows - 32, 1.0, 0.0)
    heads = k_ref.shape[1] // HD
    for i, (ref, send_ref) in enumerate(((k_ref, send_k_ref), (v_ref, send_v_ref))):
        group = (mid / P1, far / P2) if i == 0 else (mid, far)
        take = jnp.where(rows < 32, group[0], group[1]).astype(BF)
        fars = []
        for b in range(TOK // BLK):
            pooled = jnp.dot(
                take, ref[b * BLK : (b + 1) * BLK, :], preferred_element_type=jnp.float32
            )
            mids = pooled[:32].astype(BF)
            for h in range(heads):
                piece = mids[:, h * HD : (h + 1) * HD]
                send_ref[h, BLK + b * MIDB : BLK + (b + 1) * MIDB, :] = piece
                if b >= 4:
                    mid2_ref[h, i, (b - 4) * MIDB : (b - 3) * MIDB, :] = piece
            fars.append(pooled[32:36])
        fars = jnp.concatenate(fars, axis=0).astype(BF)
        for h in range(heads):
            send_ref[h, :BLK, :] = ref[TOK - BLK :, h * HD : (h + 1) * HD]
            far_ref[h, i] = fars[:, h * HD : (h + 1) * HD]


def pool(first, heads, key_rows, value_rows):
    step = 2
    return pl.pallas_call(
        pool_kernel,
        grid=(heads // step,),
        in_specs=[pl.BlockSpec((TOK, step * HD), lambda i: (0, first // step + i))] * 2,
        out_specs=[
            pl.BlockSpec((step, 2 * BLK, HD), lambda i: (i, 0, 0)),
            pl.BlockSpec((step, 2 * BLK, HD), lambda i: (i, 0, 0)),
            pl.BlockSpec((step, 2, 128, HD), lambda i: (i, 0, 0, 0)),
            pl.BlockSpec((step, 2, FARD, HD), lambda i: (i, 0, 0, 0)),
        ],
        out_shape=[
            jax.ShapeDtypeStruct((heads, 2 * BLK, HD), BF),
            jax.ShapeDtypeStruct((heads, 2 * BLK, HD), BF),
            jax.ShapeDtypeStruct((heads, 2, 128, HD), BF),
            jax.ShapeDtypeStruct((heads, 2, FARD, HD), BF),
        ],
        compiler_params=pltpu.CompilerParams(vmem_limit_bytes=VMEM_LIMIT),
        cost_estimate=pl.CostEstimate(
            flops=2 * 2 * TOK * heads * HD * 48,
            bytes_accessed=2 * TOK * heads * HD * 3,
            transcendentals=0,
        ),
        name="pool",
    )(key_rows, value_rows)


def dot_nt(a, b):
    return lax.dot_general(a, b, (((1,), (1,)), ((), ())), preferred_element_type=jnp.float32)


def dot_ones(weights, values, one):
    wide = jnp.concatenate([values, jnp.full(values.shape, one, BF)], axis=1)
    return jnp.dot(weights, wide, preferred_element_type=jnp.float32)


def attend_kernel(
    info_ref, q_ref, k_ref, v_ref, kp_ref, vp_ref, far_ok_ref, own_k_ref, own_v_ref, back_k_ref, back_v_ref, back2_ref,
    h0_ref, h1_ref, h2_ref, h3_ref, oa_ref, ob_ref, kn, vn, km, vm, sa, sb,
):
    s = info_ref[0]
    half = info_ref[1]
    flip = info_ref[2]

    far_refs = (h0_ref, h1_ref, h2_ref, h3_ref)
    from_other = jnp.full((BLK, HD), half, jnp.int32) == 0
    kn[:BLK, :] = jnp.where(from_other, back_k_ref[0, :BLK], kp_ref[...])
    vn[:BLK, :] = jnp.where(from_other, back_v_ref[0, :BLK], vp_ref[...])
    kn[BLK:, :] = k_ref[...]
    vn[BLK:, :] = v_ref[...]
    for i, (to, back_ref, own_ref) in enumerate(
        ((km, back_k_ref, own_k_ref), (vm, back_v_ref, own_v_ref))
    ):
        to[0:128, :] = back2_ref[0, i]
        to[128:384, :] = back_ref[0, BLK:]
        to[384:608, :] = own_ref[0, BLK : BLK + 224]

    def block_of(n):
        return 2 * ((n // 2) ^ flip) + n % 2

    def scores(n, s_ref):
        local = block_of(n)
        j = half * 4 + local
        start = pl.multiple_of(local * BLK, BLK)
        q = q_ref[pl.ds(start, BLK), :]
        sn = dot_nt(q, kn[pl.ds(start, BLK), :])
        sn = sn + jnp.where((s == 0) & (j == 0), NEG, 0.0)
        s_ref[:, 0:256] = sn
        top = jnp.maximum(sn[:, :128], sn[:, 128:])
        rows = lax.broadcasted_iota(jnp.int32, (BLK, BLK), 0)
        cols = lax.broadcasted_iota(jnp.int32, (BLK, BLK), 1)
        sd = dot_nt(q, kn[pl.ds(start + BLK, BLK), :])
        sd = jnp.where(cols <= rows, sd, NEG)
        s_ref[:, 256:512] = sd
        top = jnp.maximum(top, jnp.maximum(sd[:, :128], sd[:, 128:]))
        col = lax.broadcasted_iota(jnp.int32, (1, 384), 1)
        ok = jnp.minimum(col - MIDB * (R1 - 8 * s - j), (R1 - 1) * MIDB - 1 - col) >= 0
        sm = dot_nt(q, km[pl.ds(pl.multiple_of(j * MIDB, MIDB), 384), :])
        sm = sm + jnp.where(ok, 0.0, NEG)
        s_ref[:, 512:896] = sm
        for i in range(3):
            top = jnp.maximum(top, sm[:, i * 128 : i * 128 + 128])
        for i in range(4):
            sf = dot_nt(q, far_refs[i][0, 0]) + far_ok_ref[pl.ds(j, 1), i * 256 : i * 256 + 256]
            s_ref[:, 896 + i * 256 : 1152 + i * 256] = sf
            top = jnp.maximum(top, jnp.maximum(sf[:, :128], sf[:, 128:]))
        return jnp.max(top, axis=1, keepdims=True)

    def finish(n, s_ref, top, o_ref):
        local = block_of(n)
        j = half * 4 + local
        start = pl.multiple_of(local * BLK, BLK)

        def weights(a, b):
            return jnp.exp2((s_ref[:, a:b] - top) * EXP_SCALE).astype(BF)

        acc = dot_ones(weights(0, 512), vn[pl.ds(start, 512), :], 1)
        mids = vm[pl.ds(pl.multiple_of(j * MIDB, MIDB), 384), :]
        acc = acc + dot_ones(weights(512, 896), mids, P1)
        for i in range(4):
            acc = acc + dot_ones(weights(896 + i * 256, 1152 + i * 256), far_refs[i][0, 1], P2)
        at = (n % 2) * BLK
        o_ref[at : at + BLK, :] = (acc[:, :HD] / acc[:, HD:]).astype(BF)

    slots = (sa, sb)
    top = scores(0, sa)
    for n in range(4):
        later = scores(n + 1, slots[(n + 1) % 2]) if n < 3 else None
        finish(n, slots[n % 2], top, (oa_ref, ob_ref)[n // 2])
        top = later


def attend(work, first, heads, info, queries, key_rows, value_rows, far_ok, own_k, own_v, back_k, back_v, back2, *fars):
    def rows(count, row):
        return pl.BlockSpec((count, HD), lambda h, info: (row(info), first + h))

    half = rows(1024, lambda info: info[1])
    before = rows(BLK, lambda info: 3 * info[1])
    head = lambda count: pl.BlockSpec((1, 2, count, HD), lambda h, info: (h, 0, 0, 0))
    out = pl.BlockSpec((512, HD), lambda h, info: (0, h))
    return pl.pallas_call(
        attend_kernel,
        grid_spec=pltpu.PrefetchScalarGridSpec(
            num_scalar_prefetch=1,
            grid=(heads,),
            in_specs=[half, half, half, before, before]
            + [pl.BlockSpec((8, FARS), lambda h, info: (0, 0))]
            + [pl.BlockSpec((1, 2 * BLK, HD), lambda h, info: (first + h, 0, 0))] * 2
            + [pl.BlockSpec((1, 2 * BLK, HD), lambda h, info: (h, 0, 0))] * 2
            + [pl.BlockSpec((1, 2, 128, HD), lambda h, info: (first + h, 0, 0, 0))]
            + [head(256)] * 4,
            out_specs=[out, out],
            scratch_shapes=[
                pltpu.VMEM((1280, HD), BF),
                pltpu.VMEM((1280, HD), BF),
                pltpu.VMEM((MIDS, HD), BF),
                pltpu.VMEM((MIDS, HD), BF),
                pltpu.VMEM((BLK, KEYS), jnp.float32),
                pltpu.VMEM((BLK, KEYS), jnp.float32),
            ],
        ),
        out_shape=[jax.ShapeDtypeStruct((512, heads * HD), BF)] * 2,
        compiler_params=pltpu.CompilerParams(vmem_limit_bytes=VMEM_LIMIT),
        cost_estimate=pl.CostEstimate(
            flops=work,
            bytes_accessed=4096,
            transcendentals=0,
        ),
        name="attend",
    )(info, queries, key_rows, value_rows, key_rows, value_rows, far_ok, own_k, own_v, back_k, back_v, back2, *fars)


def place_kernel(columns, me_ref, *refs):
    count = len(columns)
    pieces, out_ref, held, in_sems, out_sems = refs[:count], *refs[count:]
    me = me_ref[0]
    loads, stores = [], []
    for i in range(count):
        loads.append(pltpu.make_async_copy(pieces[i], held[i], in_sems.at[i]))
        loads[i].start()
    for i, (k, at) in enumerate(columns):
        to = pl.multiple_of((me ^ k) * 1024 + at, HD)
        width = pieces[i].shape[1]
        stores.append(
            pltpu.make_async_copy(held[i], out_ref.at[:, pl.ds(to, width)], out_sems.at[i])
        )
        loads[i].wait()
        stores[i].start()
    for store in stores:
        store.wait()


def place(me, pieces, columns):
    count = len(pieces)
    return pl.pallas_call(
        lambda *refs: place_kernel(columns, *refs),
        in_specs=[pl.BlockSpec(memory_space=pltpu.SMEM)]
        + [pl.BlockSpec(memory_space=pl.ANY)] * count,
        out_specs=pl.BlockSpec(memory_space=pl.ANY),
        out_shape=jax.ShapeDtypeStruct((512, 4096), BF),
        scratch_shapes=[
            [pltpu.VMEM(piece.shape, BF) for piece in pieces],
            pltpu.SemaphoreType.DMA((count,)),
            pltpu.SemaphoreType.DMA((count,)),
        ],
        compiler_params=pltpu.CompilerParams(vmem_limit_bytes=VMEM_LIMIT),
        cost_estimate=pl.CostEstimate(
            flops=0, bytes_accessed=count * 1024 * 1024, transcendentals=0
        ),
        name="place",
    )(me, *pieces)


def swap_heads(piece, k):
    return lax.ppermute(piece, "head", [(i, i ^ k) for i in range(4)])


def far_bias(s):
    x, z, y = s // 16, (s // 4) % 4, s % 4
    of = jnp.array(FROM, jnp.int32)
    zs = ((z + of) % 4).reshape(4, 1, 1, 1)
    ys = ((y + of) % 4).reshape(1, 4, 1, 1)
    xs = (x ^ jnp.arange(2, dtype=jnp.int32)).reshape(1, 1, 2, 1)
    group = (xs * 16 + zs * 4 + ys) * FARD + jnp.arange(FARD, dtype=jnp.int32)
    limit = (8 * s + jnp.arange(8, dtype=jnp.int32) - R1) * (BLK // P2)
    return jnp.where(group.reshape(1, FARS) < limit[:, None], 0.0, NEG)


def shards(queries, key_rows, value_rows):
    s = lax.axis_index("seq").astype(jnp.int32)
    me = lax.axis_index("head").astype(jnp.int32)
    pair, flip = me // 2, me % 2
    over = lambda value, route: lax.ppermute(value, "seq", route)
    firsts = [sum(CHUNKS[:c]) for c in range(len(CHUNKS))]
    own_k, own_v, last, f0 = pool(0, HEADS, key_rows, value_rows)
    g0 = jnp.concatenate([f0, over(f0, X_ROUTE)], axis=2)
    g0, own_v = lax.optimization_barrier((g0, own_v))
    cut = lambda value, c: value[firsts[c] : firsts[c] + CHUNKS[c]]
    above = [over(cut(own_v, c), UP_Z) for c in range(2)]
    g1, g3 = over(g0, Y_DOWN), over(g0, Y_UP)
    gs = [g0, g1, g3, over(g1, Y_DOWN)]
    gs, above[0], own_k, own_v, last = lax.optimization_barrier(
        (gs, above[0], own_k, own_v, last)
    )
    own = (own_k, own_v)
    far_ok = far_bias(s)

    def first_stage(c, own_k, own_v, gs):
        h0 = jnp.concatenate([cut(g, c) for g in gs], axis=2)
        h1, h3 = over(h0, Z_DOWN), over(h0, Z_UP)
        back_k = over(cut(own_k, c), shift_route(1))
        along = over(cut(own_v, c), ALONG_Y)
        return h0, h1, h3, back_k, along

    def second_stage(above, h0, h1, h3, back_k, along):
        h2 = over(h1, Z_DOWN)
        back_v = jnp.where(s % 4 == 0, over(above, ROUND_Y), along)
        return (far_ok, *own, back_k, back_v, back2, h0, h1, h3, h2)

    pieces = {}

    def run(c, half, parts):
        which, names = ((1 - pair, (2, 3)), (pair, (0, 1)))[half]
        info = jnp.stack([s, which, flip])
        work = WORK if c else 1
        outs = attend(work, firsts[c], CHUNKS[c], info, queries, key_rows, value_rows, *parts)
        for k, out in zip(names, outs):
            pieces[c, k] = swap_heads(out, k) if k else out
        return outs[0]

    stage = first_stage(0, own_k, own_v, gs)
    back2 = over(last, shift_route(2))
    sent, h1 = lax.optimization_barrier(((own_k, own_v, gs), stage[1]))
    parts = second_stage(above[0], stage[0], h1, *stage[2:])
    stage = first_stage(1, *sent)
    done = run(0, 0, parts)
    parts_b = second_stage(above[1], *stage)
    far_ok, done = lax.optimization_barrier((parts[0], done))
    done = run(0, 1, (far_ok, *parts[1:]))
    far_ok, done, pieces[0, 2] = lax.optimization_barrier((parts_b[0], done, pieces[0, 2]))
    done = run(1, 0, (far_ok, *parts_b[1:]))
    far_ok, done, pieces[0, 3] = lax.optimization_barrier((far_ok, done, pieces[0, 3]))
    run(1, 1, (far_ok, *parts_b[1:]))
    order = sorted(pieces, key=lambda at: (at[0], at[1]))
    return place(
        me.reshape(1), [pieces[at] for at in order], [(k, firsts[c] * HD) for c, k in order]
    )


def solution(mesh):
    return jax.shard_map(
        shards,
        mesh=mesh,
        in_specs=(P("seq", "head"), P("seq", "head"), P("seq", "head")),
        out_specs=P(("seq", "head"), None),
        check_vma=False,
    )
```

```python
import math

import jax
import jax.numpy as jnp
from jax import lax
from jax.experimental import pallas as pl
from jax.experimental.pallas import tpu as pltpu
from jax.sharding import PartitionSpec as P

HD = 128
BLK = 256
P1 = 8
P2 = 64
R1 = 12
SEQ = 32
TOK = 2048
HEADS = 8
NEG = -1e30
MIDB = BLK // P1
FARD = TOK // P2
FARS = SEQ * FARD
MIDS = 19 * MIDB
KEYS = 512 + 384 + FARS
EXP_SCALE = math.log2(math.e) / math.sqrt(HD)
CHUNKS = (4, 4)
VMEM_LIMIT = 56 * 1024 * 1024
BF = jnp.bfloat16


def seq_route(move):
    route = []
    for s in range(SEQ):
        x, z, y = move(s // 16, (s // 4) % 4, s % 4)
        route.append((s, x * 16 + (z % 4) * 4 + y % 4))
    return route


Y_UP = seq_route(lambda x, z, y: (x, z, y + 1))
Y_DOWN = seq_route(lambda x, z, y: (x, z, y - 1))
X_ROUTE = seq_route(lambda x, z, y: (1 - x, z, y))
Z_UP = seq_route(lambda x, z, y: (x, z + 1, y))
Z_DOWN = seq_route(lambda x, z, y: (x, z - 1, y))
FROM = (0, 1, 3, 2)


def shift_route(distance):
    return [(i - distance, i) for i in range(distance, SEQ)]


ALONG_Y = [(i, i + 1) for i in range(SEQ) if i % 4 < 3]
UP_Z = [(i, i + 4) for i in range(3, SEQ - 4, 4)]
ROUND_Y = [(i, i - 3) for i in range(7, SEQ, 4)]


def pool_kernel(k_ref, v_ref, send_k_ref, send_v_ref, mid2_ref, far_ref):
    rows = lax.broadcasted_iota(jnp.int32, (48, BLK), 0)
    cols = lax.broadcasted_iota(jnp.int32, (48, BLK), 1)
    mid = jnp.where(cols // P1 == rows, 1.0, 0.0)
    far = jnp.where(cols // P2 == rows - 32, 1.0, 0.0)
    heads = k_ref.shape[1] // HD
    for i, (ref, send_ref) in enumerate(((k_ref, send_k_ref), (v_ref, send_v_ref))):
        group = (mid / P1, far / P2) if i == 0 else (mid, far)
        take = jnp.where(rows < 32, group[0], group[1]).astype(BF)
        fars = []
        for b in range(TOK // BLK):
            pooled = jnp.dot(
                take, ref[b * BLK : (b + 1) * BLK, :], preferred_element_type=jnp.float32
            )
            mids = pooled[:32].astype(BF)
            for h in range(heads):
                piece = mids[:, h * HD : (h + 1) * HD]
                send_ref[h, BLK + b * MIDB : BLK + (b + 1) * MIDB, :] = piece
                if b >= 4:
                    mid2_ref[h, i, (b - 4) * MIDB : (b - 3) * MIDB, :] = piece
            fars.append(pooled[32:36])
        fars = jnp.concatenate(fars, axis=0).astype(BF)
        for h in range(heads):
            send_ref[h, :BLK, :] = ref[TOK - BLK :, h * HD : (h + 1) * HD]
            far_ref[h, i] = fars[:, h * HD : (h + 1) * HD]


def pool(first, heads, key_rows, value_rows):
    step = 2
    return pl.pallas_call(
        pool_kernel,
        grid=(heads // step,),
        in_specs=[pl.BlockSpec((TOK, step * HD), lambda i: (0, first // step + i))] * 2,
        out_specs=[
            pl.BlockSpec((step, 2 * BLK, HD), lambda i: (i, 0, 0)),
            pl.BlockSpec((step, 2 * BLK, HD), lambda i: (i, 0, 0)),
            pl.BlockSpec((step, 2, 128, HD), lambda i: (i, 0, 0, 0)),
            pl.BlockSpec((step, 2, FARD, HD), lambda i: (i, 0, 0, 0)),
        ],
        out_shape=[
            jax.ShapeDtypeStruct((heads, 2 * BLK, HD), BF),
            jax.ShapeDtypeStruct((heads, 2 * BLK, HD), BF),
            jax.ShapeDtypeStruct((heads, 2, 128, HD), BF),
            jax.ShapeDtypeStruct((heads, 2, FARD, HD), BF),
        ],
        compiler_params=pltpu.CompilerParams(vmem_limit_bytes=VMEM_LIMIT),
        cost_estimate=pl.CostEstimate(
            flops=2 * 2 * TOK * heads * HD * 48,
            bytes_accessed=2 * TOK * heads * HD * 3,
            transcendentals=0,
        ),
        name="pool",
    )(key_rows, value_rows)


def dot_nt(a, b):
    return lax.dot_general(a, b, (((1,), (1,)), ((), ())), preferred_element_type=jnp.float32)


def dot_ones(weights, values, one):
    wide = jnp.concatenate([values, jnp.full(values.shape, one, BF)], axis=1)
    return jnp.dot(weights, wide, preferred_element_type=jnp.float32)


def attend_kernel(
    info_ref, q_ref, k_ref, v_ref, kp_ref, vp_ref, far_ok_ref, own_k_ref, own_v_ref, back_k_ref, back_v_ref, back2_ref,
    h0_ref, h1_ref, h2_ref, h3_ref, oa_ref, ob_ref, kn, vn, km, vm, sa, sb,
):
    s = info_ref[0]
    half = info_ref[1]
    flip = info_ref[2]

    far_refs = (h0_ref, h1_ref, h2_ref, h3_ref)
    from_other = jnp.full((BLK, HD), half, jnp.int32) == 0
    kn[:BLK, :] = jnp.where(from_other, back_k_ref[0, :BLK], kp_ref[...])
    vn[:BLK, :] = jnp.where(from_other, back_v_ref[0, :BLK], vp_ref[...])
    kn[BLK:, :] = k_ref[...]
    vn[BLK:, :] = v_ref[...]
    for i, (to, back_ref, own_ref) in enumerate(
        ((km, back_k_ref, own_k_ref), (vm, back_v_ref, own_v_ref))
    ):
        to[0:128, :] = back2_ref[0, i]
        to[128:384, :] = back_ref[0, BLK:]
        to[384:608, :] = own_ref[0, BLK : BLK + 224]

    def block_of(n):
        return 2 * ((n // 2) ^ flip) + n % 2

    def scores(n, s_ref):
        local = block_of(n)
        j = half * 4 + local
        start = pl.multiple_of(local * BLK, BLK)
        q = q_ref[pl.ds(start, BLK), :]
        sn = dot_nt(q, kn[pl.ds(start, BLK), :])
        sn = sn + jnp.where((s == 0) & (j == 0), NEG, 0.0)
        s_ref[:, 0:256] = sn
        top = jnp.maximum(sn[:, :128], sn[:, 128:])
        rows = lax.broadcasted_iota(jnp.int32, (BLK, BLK), 0)
        cols = lax.broadcasted_iota(jnp.int32, (BLK, BLK), 1)
        sd = dot_nt(q, kn[pl.ds(start + BLK, BLK), :])
        sd = jnp.where(cols <= rows, sd, NEG)
        s_ref[:, 256:512] = sd
        top = jnp.maximum(top, jnp.maximum(sd[:, :128], sd[:, 128:]))
        col = lax.broadcasted_iota(jnp.int32, (1, 384), 1)
        ok = jnp.minimum(col - MIDB * (R1 - 8 * s - j), (R1 - 1) * MIDB - 1 - col) >= 0
        sm = dot_nt(q, km[pl.ds(pl.multiple_of(j * MIDB, MIDB), 384), :])
        sm = sm + jnp.where(ok, 0.0, NEG)
        s_ref[:, 512:896] = sm
        for i in range(3):
            top = jnp.maximum(top, sm[:, i * 128 : i * 128 + 128])
        for i in range(4):
            sf = dot_nt(q, far_refs[i][0, 0]) + far_ok_ref[pl.ds(j, 1), i * 256 : i * 256 + 256]
            s_ref[:, 896 + i * 256 : 1152 + i * 256] = sf
            top = jnp.maximum(top, jnp.maximum(sf[:, :128], sf[:, 128:]))
        return jnp.max(top, axis=1, keepdims=True)

    def finish(n, s_ref, top, o_ref):
        local = block_of(n)
        j = half * 4 + local
        start = pl.multiple_of(local * BLK, BLK)

        def weights(a, b):
            return jnp.exp2((s_ref[:, a:b] - top) * EXP_SCALE).astype(BF)

        acc = dot_ones(weights(0, 512), vn[pl.ds(start, 512), :], 1)
        mids = vm[pl.ds(pl.multiple_of(j * MIDB, MIDB), 384), :]
        acc = acc + dot_ones(weights(512, 896), mids, P1)
        for i in range(4):
            acc = acc + dot_ones(weights(896 + i * 256, 1152 + i * 256), far_refs[i][0, 1], P2)
        at = (n % 2) * BLK
        o_ref[at : at + BLK, :] = (acc[:, :HD] / acc[:, HD:]).astype(BF)

    slots = (sa, sb)
    top = scores(0, sa)
    for n in range(4):
        later = scores(n + 1, slots[(n + 1) % 2]) if n < 3 else None
        finish(n, slots[n % 2], top, (oa_ref, ob_ref)[n // 2])
        top = later


def attend(first, heads, info, queries, key_rows, value_rows, far_ok, own_k, own_v, back_k, back_v, back2, *fars):
    def rows(count, row):
        return pl.BlockSpec((count, HD), lambda h, info: (row(info), first + h))

    half = rows(1024, lambda info: info[1])
    before = rows(BLK, lambda info: 3 * info[1])
    head = lambda count: pl.BlockSpec((1, 2, count, HD), lambda h, info: (first + h, 0, 0, 0))
    out = pl.BlockSpec((512, HD), lambda h, info: (0, h))
    return pl.pallas_call(
        attend_kernel,
        grid_spec=pltpu.PrefetchScalarGridSpec(
            num_scalar_prefetch=1,
            grid=(heads,),
            in_specs=[half, half, half, before, before]
            + [pl.BlockSpec((8, FARS), lambda h, info: (0, 0))]
            + [pl.BlockSpec((1, 2 * BLK, HD), lambda h, info: (first + h, 0, 0))] * 4
            + [head(128)]
            + [head(256)] * 4,
            out_specs=[out, out],
            scratch_shapes=[
                pltpu.VMEM((1280, HD), BF),
                pltpu.VMEM((1280, HD), BF),
                pltpu.VMEM((MIDS, HD), BF),
                pltpu.VMEM((MIDS, HD), BF),
                pltpu.VMEM((BLK, KEYS), jnp.float32),
                pltpu.VMEM((BLK, KEYS), jnp.float32),
            ],
        ),
        out_shape=[jax.ShapeDtypeStruct((512, heads * HD), BF)] * 2,
        compiler_params=pltpu.CompilerParams(vmem_limit_bytes=VMEM_LIMIT),
        cost_estimate=pl.CostEstimate(
            flops=heads * 4 * BLK * KEYS * HD * 8,
            bytes_accessed=heads * HD * 2 * 6000,
            transcendentals=heads * 4 * BLK * KEYS,
        ),
        name="attend",
    )(info, queries, key_rows, value_rows, key_rows, value_rows, far_ok, own_k, own_v, back_k, back_v, back2, *fars)


def place_kernel(columns, me_ref, *refs):
    count = len(columns)
    pieces, out_ref, held, in_sems, out_sems = refs[:count], *refs[count:]
    me = me_ref[0]
    loads, stores = [], []
    for i in range(count):
        loads.append(pltpu.make_async_copy(pieces[i], held[i], in_sems.at[i]))
        loads[i].start()
    for i, (k, at) in enumerate(columns):
        to = pl.multiple_of((me ^ k) * 1024 + at, HD)
        width = pieces[i].shape[1]
        stores.append(
            pltpu.make_async_copy(held[i], out_ref.at[:, pl.ds(to, width)], out_sems.at[i])
        )
        loads[i].wait()
        stores[i].start()
    for store in stores:
        store.wait()


def place(me, pieces, columns):
    count = len(pieces)
    return pl.pallas_call(
        lambda *refs: place_kernel(columns, *refs),
        in_specs=[pl.BlockSpec(memory_space=pltpu.SMEM)]
        + [pl.BlockSpec(memory_space=pl.ANY)] * count,
        out_specs=pl.BlockSpec(memory_space=pl.ANY),
        out_shape=jax.ShapeDtypeStruct((512, 4096), BF),
        scratch_shapes=[
            [pltpu.VMEM(piece.shape, BF) for piece in pieces],
            pltpu.SemaphoreType.DMA((count,)),
            pltpu.SemaphoreType.DMA((count,)),
        ],
        compiler_params=pltpu.CompilerParams(vmem_limit_bytes=VMEM_LIMIT),
        cost_estimate=pl.CostEstimate(
            flops=0, bytes_accessed=count * 1024 * 1024, transcendentals=0
        ),
        name="place",
    )(me, *pieces)


def swap_heads(piece, k):
    return lax.ppermute(piece, "head", [(i, i ^ k) for i in range(4)])


def far_bias(s):
    x, z, y = s // 16, (s // 4) % 4, s % 4
    of = jnp.array(FROM, jnp.int32)
    zs = ((z + of) % 4).reshape(4, 1, 1, 1)
    ys = ((y + of) % 4).reshape(1, 4, 1, 1)
    xs = (x ^ jnp.arange(2, dtype=jnp.int32)).reshape(1, 1, 2, 1)
    group = (xs * 16 + zs * 4 + ys) * FARD + jnp.arange(FARD, dtype=jnp.int32)
    limit = (8 * s + jnp.arange(8, dtype=jnp.int32) - R1) * (BLK // P2)
    return jnp.where(group.reshape(1, FARS) < limit[:, None], 0.0, NEG)


def shards(queries, key_rows, value_rows):
    s = lax.axis_index("seq").astype(jnp.int32)
    me = lax.axis_index("head").astype(jnp.int32)
    pair, flip = me // 2, me % 2
    over = lambda value, route: lax.ppermute(value, "seq", route)
    firsts = [sum(CHUNKS[:c]) for c in range(len(CHUNKS))]
    own_k, own_v, last, f0 = pool(0, HEADS, key_rows, value_rows)
    g0 = jnp.concatenate([f0, over(f0, X_ROUTE)], axis=2)
    g0, own_v = lax.optimization_barrier((g0, own_v))
    above = over(own_v, UP_Z)
    g1, g3 = over(g0, Y_DOWN), over(g0, Y_UP)
    g1, g3, own_k, last = lax.optimization_barrier((g1, g3, own_k, last))
    back2 = over(last, shift_route(2))
    gs = [g0, g1, g3, over(g1, Y_DOWN)]
    own_v, gs, above, back2 = lax.optimization_barrier((own_v, gs, above, back2))
    back_k = over(own_k, shift_route(1))
    back_v = jnp.where(s % 4 == 0, over(above, ROUND_Y), over(own_v, ALONG_Y))
    h0 = jnp.concatenate(gs, axis=2)
    h1, h3 = over(h0, Z_DOWN), over(h0, Z_UP)
    h1, back_k = lax.optimization_barrier((h1, back_k))
    fars = [h0, h1, h3, over(h1, Z_DOWN)]
    parts = (far_bias(s), own_k, own_v, back_k, back_v, back2, *fars)
    pieces = {}
    args = (queries, key_rows, value_rows)
    for which, names in ((1 - pair, (2, 3)), (pair, (0, 1))):
        for c, (first, heads) in enumerate(zip(firsts, CHUNKS)):
            outs = attend(first, heads, jnp.stack([s, which, flip]), *args, *parts)
            for k, out in zip(names, outs):
                pieces[c, k] = swap_heads(out, k) if k else out
            args = lax.optimization_barrier((*args, outs[0]))[:3]
    order = sorted(pieces, key=lambda at: (at[0], at[1]))
    return place(
        me.reshape(1), [pieces[at] for at in order], [(k, firsts[c] * HD) for c, k in order]
    )


def solution(mesh):
    return jax.shard_map(
        shards,
        mesh=mesh,
        in_specs=(P("seq", "head"), P("seq", "head"), P("seq", "head")),
        out_specs=P(("seq", "head"), None),
        check_vma=False,
    )
```

```python
import math

import jax
import jax.numpy as jnp
from jax import lax
from jax.experimental import pallas as pl
from jax.experimental.pallas import tpu as pltpu
from jax.sharding import PartitionSpec as P

HD = 128
BLK = 256
P1 = 8
P2 = 64
R1 = 12
SEQ = 32
TOK = 2048
HEADS = 8
NEG = -1e30
MIDB = BLK // P1
FARD = TOK // P2
FARS = SEQ * FARD
MIDS = 19 * MIDB
KEYS = 512 + 384 + FARS
EXP_SCALE = math.log2(math.e) / math.sqrt(HD)
CHUNKS = (4, 4)
VMEM_LIMIT = 56 * 1024 * 1024
BF = jnp.bfloat16


def seq_route(move):
    route = []
    for s in range(SEQ):
        x, z, y = move(s // 16, (s // 4) % 4, s % 4)
        route.append((s, x * 16 + (z % 4) * 4 + y % 4))
    return route


Y_UP = seq_route(lambda x, z, y: (x, z, y + 1))
Y_DOWN = seq_route(lambda x, z, y: (x, z, y - 1))
X_ROUTE = seq_route(lambda x, z, y: (1 - x, z, y))
Z_UP = seq_route(lambda x, z, y: (x, z + 1, y))
Z_DOWN = seq_route(lambda x, z, y: (x, z - 1, y))
FROM = (0, 1, 3, 2)


def shift_route(distance):
    return [(i - distance, i) for i in range(distance, SEQ)]


ALONG_Y = [(i, i + 1) for i in range(SEQ) if i % 4 < 3]
UP_Z = [(i, i + 4) for i in range(3, SEQ - 4, 4)]
ROUND_Y = [(i, i - 3) for i in range(7, SEQ, 4)]


def pool_kernel(k_ref, v_ref, send_k_ref, send_v_ref, mid2_ref, far_ref):
    rows = lax.broadcasted_iota(jnp.int32, (48, BLK), 0)
    cols = lax.broadcasted_iota(jnp.int32, (48, BLK), 1)
    mid = jnp.where(cols // P1 == rows, 1.0, 0.0)
    far = jnp.where(cols // P2 == rows - 32, 1.0, 0.0)
    heads = k_ref.shape[1] // HD
    for i, (ref, send_ref) in enumerate(((k_ref, send_k_ref), (v_ref, send_v_ref))):
        group = (mid / P1, far / P2) if i == 0 else (mid, far)
        take = jnp.where(rows < 32, group[0], group[1]).astype(BF)
        fars = []
        for b in range(TOK // BLK):
            pooled = jnp.dot(
                take, ref[b * BLK : (b + 1) * BLK, :], preferred_element_type=jnp.float32
            )
            mids = pooled[:32].astype(BF)
            for h in range(heads):
                piece = mids[:, h * HD : (h + 1) * HD]
                send_ref[h, BLK + b * MIDB : BLK + (b + 1) * MIDB, :] = piece
                if b >= 4:
                    mid2_ref[h, i, (b - 4) * MIDB : (b - 3) * MIDB, :] = piece
            fars.append(pooled[32:36])
        fars = jnp.concatenate(fars, axis=0).astype(BF)
        for h in range(heads):
            send_ref[h, :BLK, :] = ref[TOK - BLK :, h * HD : (h + 1) * HD]
            far_ref[h, i] = fars[:, h * HD : (h + 1) * HD]


def pool(first, heads, key_rows, value_rows):
    step = 2
    return pl.pallas_call(
        pool_kernel,
        grid=(heads // step,),
        in_specs=[pl.BlockSpec((TOK, step * HD), lambda i: (0, first // step + i))] * 2,
        out_specs=[
            pl.BlockSpec((step, 2 * BLK, HD), lambda i: (i, 0, 0)),
            pl.BlockSpec((step, 2 * BLK, HD), lambda i: (i, 0, 0)),
            pl.BlockSpec((step, 2, 128, HD), lambda i: (i, 0, 0, 0)),
            pl.BlockSpec((step, 2, FARD, HD), lambda i: (i, 0, 0, 0)),
        ],
        out_shape=[
            jax.ShapeDtypeStruct((heads, 2 * BLK, HD), BF),
            jax.ShapeDtypeStruct((heads, 2 * BLK, HD), BF),
            jax.ShapeDtypeStruct((heads, 2, 128, HD), BF),
            jax.ShapeDtypeStruct((heads, 2, FARD, HD), BF),
        ],
        compiler_params=pltpu.CompilerParams(vmem_limit_bytes=VMEM_LIMIT),
        cost_estimate=pl.CostEstimate(
            flops=2 * 2 * TOK * heads * HD * 48,
            bytes_accessed=2 * TOK * heads * HD * 3,
            transcendentals=0,
        ),
        name="pool",
    )(key_rows, value_rows)


def dot_nt(a, b):
    return lax.dot_general(a, b, (((1,), (1,)), ((), ())), preferred_element_type=jnp.float32)


def dot_ones(weights, values, one):
    wide = jnp.concatenate([values, jnp.full(values.shape, one, BF)], axis=1)
    return jnp.dot(weights, wide, preferred_element_type=jnp.float32)


def attend_kernel(
    info_ref, q_ref, k_ref, v_ref, kp_ref, vp_ref, far_ok_ref, own_k_ref, own_v_ref, back_k_ref, back_v_ref, back2_ref,
    h0_ref, h1_ref, h2_ref, h3_ref, oa_ref, ob_ref, kn, vn, km, vm, sa, sb,
):
    s = info_ref[0]
    half = info_ref[1]
    flip = info_ref[2]

    far_refs = (h0_ref, h1_ref, h2_ref, h3_ref)
    from_other = jnp.full((BLK, HD), half, jnp.int32) == 0
    kn[:BLK, :] = jnp.where(from_other, back_k_ref[0, :BLK], kp_ref[...])
    vn[:BLK, :] = jnp.where(from_other, back_v_ref[0, :BLK], vp_ref[...])
    kn[BLK:, :] = k_ref[...]
    vn[BLK:, :] = v_ref[...]
    for i, (to, back_ref, own_ref) in enumerate(
        ((km, back_k_ref, own_k_ref), (vm, back_v_ref, own_v_ref))
    ):
        to[0:128, :] = back2_ref[0, i]
        to[128:384, :] = back_ref[0, BLK:]
        to[384:608, :] = own_ref[0, BLK : BLK + 224]

    def block_of(n):
        return 2 * ((n // 2) ^ flip) + n % 2

    def scores(n, s_ref):
        local = block_of(n)
        j = half * 4 + local
        start = pl.multiple_of(local * BLK, BLK)
        q = q_ref[pl.ds(start, BLK), :]
        sn = dot_nt(q, kn[pl.ds(start, BLK), :])
        sn = sn + jnp.where((s == 0) & (j == 0), NEG, 0.0)
        s_ref[:, 0:256] = sn
        top = jnp.maximum(sn[:, :128], sn[:, 128:])
        rows = lax.broadcasted_iota(jnp.int32, (BLK, BLK), 0)
        cols = lax.broadcasted_iota(jnp.int32, (BLK, BLK), 1)
        sd = dot_nt(q, kn[pl.ds(start + BLK, BLK), :])
        sd = jnp.where(cols <= rows, sd, NEG)
        s_ref[:, 256:512] = sd
        top = jnp.maximum(top, jnp.maximum(sd[:, :128], sd[:, 128:]))
        col = lax.broadcasted_iota(jnp.int32, (1, 384), 1)
        ok = jnp.minimum(col - MIDB * (R1 - 8 * s - j), (R1 - 1) * MIDB - 1 - col) >= 0
        sm = dot_nt(q, km[pl.ds(pl.multiple_of(j * MIDB, MIDB), 384), :])
        sm = sm + jnp.where(ok, 0.0, NEG)
        s_ref[:, 512:896] = sm
        for i in range(3):
            top = jnp.maximum(top, sm[:, i * 128 : i * 128 + 128])
        for i in range(4):
            sf = dot_nt(q, far_refs[i][0, 0]) + far_ok_ref[pl.ds(j, 1), i * 256 : i * 256 + 256]
            s_ref[:, 896 + i * 256 : 1152 + i * 256] = sf
            top = jnp.maximum(top, jnp.maximum(sf[:, :128], sf[:, 128:]))
        return jnp.max(top, axis=1, keepdims=True)

    def finish(n, s_ref, top, o_ref):
        local = block_of(n)
        j = half * 4 + local
        start = pl.multiple_of(local * BLK, BLK)

        def weights(a, b):
            return jnp.exp2((s_ref[:, a:b] - top) * EXP_SCALE).astype(BF)

        acc = dot_ones(weights(0, 512), vn[pl.ds(start, 512), :], 1)
        mids = vm[pl.ds(pl.multiple_of(j * MIDB, MIDB), 384), :]
        acc = acc + dot_ones(weights(512, 896), mids, P1)
        for i in range(4):
            acc = acc + dot_ones(weights(896 + i * 256, 1152 + i * 256), far_refs[i][0, 1], P2)
        at = (n % 2) * BLK
        o_ref[at : at + BLK, :] = (acc[:, :HD] / acc[:, HD:]).astype(BF)

    slots = (sa, sb)
    top = scores(0, sa)
    for n in range(4):
        later = scores(n + 1, slots[(n + 1) % 2]) if n < 3 else None
        finish(n, slots[n % 2], top, (oa_ref, ob_ref)[n // 2])
        top = later


def attend(first, heads, info, queries, key_rows, value_rows, far_ok, own_k, own_v, back_k, back_v, back2, *fars):
    def rows(count, row):
        return pl.BlockSpec((count, HD), lambda h, info: (row(info), first + h))

    half = rows(1024, lambda info: info[1])
    before = rows(BLK, lambda info: 3 * info[1])
    head = lambda count: pl.BlockSpec((1, 2, count, HD), lambda h, info: (first + h, 0, 0, 0))
    out = pl.BlockSpec((512, HD), lambda h, info: (0, h))
    return pl.pallas_call(
        attend_kernel,
        grid_spec=pltpu.PrefetchScalarGridSpec(
            num_scalar_prefetch=1,
            grid=(heads,),
            in_specs=[half, half, half, before, before]
            + [pl.BlockSpec((8, FARS), lambda h, info: (0, 0))]
            + [pl.BlockSpec((1, 2 * BLK, HD), lambda h, info: (first + h, 0, 0))] * 4
            + [head(128)]
            + [head(256)] * 3
            + [pl.BlockSpec((1, 2, 256, HD), lambda h, info: (h, 0, 0, 0))],
            out_specs=[out, out],
            scratch_shapes=[
                pltpu.VMEM((1280, HD), BF),
                pltpu.VMEM((1280, HD), BF),
                pltpu.VMEM((MIDS, HD), BF),
                pltpu.VMEM((MIDS, HD), BF),
                pltpu.VMEM((BLK, KEYS), jnp.float32),
                pltpu.VMEM((BLK, KEYS), jnp.float32),
            ],
        ),
        out_shape=[jax.ShapeDtypeStruct((512, heads * HD), BF)] * 2,
        compiler_params=pltpu.CompilerParams(vmem_limit_bytes=VMEM_LIMIT),
        cost_estimate=pl.CostEstimate(
            flops=heads * 4 * BLK * KEYS * HD * 8,
            bytes_accessed=heads * HD * 2 * 6000,
            transcendentals=heads * 4 * BLK * KEYS,
        ),
        name="attend",
    )(info, queries, key_rows, value_rows, key_rows, value_rows, far_ok, own_k, own_v, back_k, back_v, back2, *fars)


def place_kernel(columns, me_ref, *refs):
    count = len(columns)
    pieces, out_ref, held, in_sems, out_sems = refs[:count], *refs[count:]
    me = me_ref[0]
    loads, stores = [], []
    for i in range(count):
        loads.append(pltpu.make_async_copy(pieces[i], held[i], in_sems.at[i]))
        loads[i].start()
    for i, (k, at) in enumerate(columns):
        to = pl.multiple_of((me ^ k) * 1024 + at, HD)
        width = pieces[i].shape[1]
        stores.append(
            pltpu.make_async_copy(held[i], out_ref.at[:, pl.ds(to, width)], out_sems.at[i])
        )
        loads[i].wait()
        stores[i].start()
    for store in stores:
        store.wait()


def place(me, pieces, columns):
    count = len(pieces)
    return pl.pallas_call(
        lambda *refs: place_kernel(columns, *refs),
        in_specs=[pl.BlockSpec(memory_space=pltpu.SMEM)]
        + [pl.BlockSpec(memory_space=pl.ANY)] * count,
        out_specs=pl.BlockSpec(memory_space=pl.ANY),
        out_shape=jax.ShapeDtypeStruct((512, 4096), BF),
        scratch_shapes=[
            [pltpu.VMEM(piece.shape, BF) for piece in pieces],
            pltpu.SemaphoreType.DMA((count,)),
            pltpu.SemaphoreType.DMA((count,)),
        ],
        compiler_params=pltpu.CompilerParams(vmem_limit_bytes=VMEM_LIMIT),
        cost_estimate=pl.CostEstimate(
            flops=0, bytes_accessed=count * 1024 * 1024, transcendentals=0
        ),
        name="place",
    )(me, *pieces)


def swap_heads(piece, k):
    return lax.ppermute(piece, "head", [(i, i ^ k) for i in range(4)])


def far_bias(s):
    x, z, y = s // 16, (s // 4) % 4, s % 4
    of = jnp.array(FROM, jnp.int32)
    zs = ((z + of) % 4).reshape(4, 1, 1, 1)
    ys = ((y + of) % 4).reshape(1, 4, 1, 1)
    xs = (x ^ jnp.arange(2, dtype=jnp.int32)).reshape(1, 1, 2, 1)
    group = (xs * 16 + zs * 4 + ys) * FARD + jnp.arange(FARD, dtype=jnp.int32)
    limit = (8 * s + jnp.arange(8, dtype=jnp.int32) - R1) * (BLK // P2)
    return jnp.where(group.reshape(1, FARS) < limit[:, None], 0.0, NEG)


def shards(queries, key_rows, value_rows):
    s = lax.axis_index("seq").astype(jnp.int32)
    me = lax.axis_index("head").astype(jnp.int32)
    pair, flip = me // 2, me % 2
    over = lambda value, route: lax.ppermute(value, "seq", route)
    firsts = [sum(CHUNKS[:c]) for c in range(len(CHUNKS))]
    own_k, own_v, last, f0 = pool(0, HEADS, key_rows, value_rows)
    g0 = jnp.concatenate([f0, over(f0, X_ROUTE)], axis=2)
    g0, own_v = lax.optimization_barrier((g0, own_v))
    above = over(own_v, UP_Z)
    g1, g3 = over(g0, Y_DOWN), over(g0, Y_UP)
    g1, g3, own_k, last = lax.optimization_barrier((g1, g3, own_k, last))
    gs = [g0, g1, g3, over(g1, Y_DOWN)]
    own_v, gs, above, last = lax.optimization_barrier((own_v, gs, above, last))
    back2 = over(last, shift_route(2))
    back_k = over(own_k, shift_route(1))
    back_v = jnp.where(s % 4 == 0, over(above, ROUND_Y), over(own_v, ALONG_Y))
    h0 = jnp.concatenate(gs, axis=2)
    h1, h3 = over(h0, Z_DOWN), over(h0, Z_UP)
    h1, back_k = lax.optimization_barrier((h1, back_k))
    h3, back2 = lax.optimization_barrier((h3, back2))
    split = CHUNKS[0]
    h2 = (over(h1[:split], Z_DOWN), over(h3[split:], Z_UP))
    parts = (far_bias(s), own_k, own_v, back_k, back_v, back2, h0, h1, h3)
    pieces = {}
    args = (queries, key_rows, value_rows)
    for which, names in ((1 - pair, (2, 3)), (pair, (0, 1))):
        for c, (first, heads) in enumerate(zip(firsts, CHUNKS)):
            outs = attend(first, heads, jnp.stack([s, which, flip]), *args, *parts, h2[c])
            for k, out in zip(names, outs):
                if (c, k) == (1, 1):
                    out, pieces[1, 2], pieces[1, 3] = lax.optimization_barrier(
                        (out, pieces[1, 2], pieces[1, 3])
                    )
                pieces[c, k] = swap_heads(out, k) if k else out
            args = lax.optimization_barrier((*args, outs[0]))[:3]
    order = sorted(pieces, key=lambda at: (at[0], at[1]))
    return place(
        me.reshape(1), [pieces[at] for at in order], [(k, firsts[c] * HD) for c, k in order]
    )


def solution(mesh):
    return jax.shard_map(
        shards,
        mesh=mesh,
        in_specs=(P("seq", "head"), P("seq", "head"), P("seq", "head")),
        out_specs=P(("seq", "head"), None),
        check_vma=False,
    )
```

```python
import math

import jax
import jax.numpy as jnp
from jax import lax
from jax.experimental import pallas as pl
from jax.experimental.pallas import tpu as pltpu
from jax.sharding import PartitionSpec as P

HD = 128
BLK = 256
P1 = 8
P2 = 64
R1 = 12
SEQ = 32
TOK = 2048
HEADS = 8
NEG = -1e30
MIDB = BLK // P1
FARD = TOK // P2
FARS = SEQ * FARD
MIDS = 19 * MIDB
KEYS = 512 + 384 + FARS
EXP_SCALE = math.log2(math.e) / math.sqrt(HD)
CHUNKS = (4, 4)
VMEM_LIMIT = 56 * 1024 * 1024
BF = jnp.bfloat16


def seq_route(move):
    route = []
    for s in range(SEQ):
        x, z, y = move(s // 16, (s // 4) % 4, s % 4)
        route.append((s, x * 16 + (z % 4) * 4 + y % 4))
    return route


Y_UP = seq_route(lambda x, z, y: (x, z, y + 1))
Y_DOWN = seq_route(lambda x, z, y: (x, z, y - 1))
X_ROUTE = seq_route(lambda x, z, y: (1 - x, z, y))
Z_UP = seq_route(lambda x, z, y: (x, z + 1, y))
Z_DOWN = seq_route(lambda x, z, y: (x, z - 1, y))
FROM = (0, 1, 3, 2)


def shift_route(distance):
    return [(i - distance, i) for i in range(distance, SEQ)]


ALONG_Y = [(i, i + 1) for i in range(SEQ) if i % 4 < 3]
UP_Z = [(i, i + 4) for i in range(3, SEQ - 4, 4)]
ROUND_Y = [(i, i - 3) for i in range(7, SEQ, 4)]


def pool_kernel(k_ref, v_ref, send_k_ref, send_v_ref, mid2_ref, far_ref):
    rows = lax.broadcasted_iota(jnp.int32, (48, BLK), 0)
    cols = lax.broadcasted_iota(jnp.int32, (48, BLK), 1)
    mid = jnp.where(cols // P1 == rows, 1.0, 0.0)
    far = jnp.where(cols // P2 == rows - 32, 1.0, 0.0)
    heads = k_ref.shape[1] // HD
    for i, (ref, send_ref) in enumerate(((k_ref, send_k_ref), (v_ref, send_v_ref))):
        group = (mid / P1, far / P2) if i == 0 else (mid, far)
        take = jnp.where(rows < 32, group[0], group[1]).astype(BF)
        fars = []
        for b in range(TOK // BLK):
            pooled = jnp.dot(
                take, ref[b * BLK : (b + 1) * BLK, :], preferred_element_type=jnp.float32
            )
            mids = pooled[:32].astype(BF)
            for h in range(heads):
                piece = mids[:, h * HD : (h + 1) * HD]
                send_ref[h, BLK + b * MIDB : BLK + (b + 1) * MIDB, :] = piece
                if b >= 4:
                    mid2_ref[h, i, (b - 4) * MIDB : (b - 3) * MIDB, :] = piece
            fars.append(pooled[32:36])
        fars = jnp.concatenate(fars, axis=0).astype(BF)
        for h in range(heads):
            send_ref[h, :BLK, :] = ref[TOK - BLK :, h * HD : (h + 1) * HD]
            far_ref[h, i] = fars[:, h * HD : (h + 1) * HD]


def pool(first, heads, key_rows, value_rows):
    step = 2
    return pl.pallas_call(
        pool_kernel,
        grid=(heads // step,),
        in_specs=[pl.BlockSpec((TOK, step * HD), lambda i: (0, first // step + i))] * 2,
        out_specs=[
            pl.BlockSpec((step, 2 * BLK, HD), lambda i: (i, 0, 0)),
            pl.BlockSpec((step, 2 * BLK, HD), lambda i: (i, 0, 0)),
            pl.BlockSpec((step, 2, 128, HD), lambda i: (i, 0, 0, 0)),
            pl.BlockSpec((step, 2, FARD, HD), lambda i: (i, 0, 0, 0)),
        ],
        out_shape=[
            jax.ShapeDtypeStruct((heads, 2 * BLK, HD), BF),
            jax.ShapeDtypeStruct((heads, 2 * BLK, HD), BF),
            jax.ShapeDtypeStruct((heads, 2, 128, HD), BF),
            jax.ShapeDtypeStruct((heads, 2, FARD, HD), BF),
        ],
        compiler_params=pltpu.CompilerParams(vmem_limit_bytes=VMEM_LIMIT),
        cost_estimate=pl.CostEstimate(
            flops=2 * 2 * TOK * heads * HD * 48,
            bytes_accessed=2 * TOK * heads * HD * 3,
            transcendentals=0,
        ),
        name="pool",
    )(key_rows, value_rows)


def dot_nt(a, b):
    return lax.dot_general(a, b, (((1,), (1,)), ((), ())), preferred_element_type=jnp.float32)


def dot_ones(weights, values, one):
    wide = jnp.concatenate([values, jnp.full(values.shape, one, BF)], axis=1)
    return jnp.dot(weights, wide, preferred_element_type=jnp.float32)


def attend_kernel(
    info_ref, q_ref, k_ref, v_ref, kp_ref, vp_ref, far_ok_ref, own_k_ref, own_v_ref, back_k_ref, back_v_ref, back2_ref,
    h0_ref, h1_ref, h2_ref, h3_ref, oa_ref, ob_ref, kn, vn, km, vm, sa, sb,
):
    s = info_ref[0]
    half = info_ref[1]
    flip = info_ref[2]

    far_refs = (h0_ref, h1_ref, h2_ref, h3_ref)
    from_other = jnp.full((BLK, HD), half, jnp.int32) == 0
    kn[:BLK, :] = jnp.where(from_other, back_k_ref[0, :BLK], kp_ref[...])
    vn[:BLK, :] = jnp.where(from_other, back_v_ref[0, :BLK], vp_ref[...])
    kn[BLK:, :] = k_ref[...]
    vn[BLK:, :] = v_ref[...]
    for i, (to, back_ref, own_ref) in enumerate(
        ((km, back_k_ref, own_k_ref), (vm, back_v_ref, own_v_ref))
    ):
        to[0:128, :] = back2_ref[0, i]
        to[128:384, :] = back_ref[0, BLK:]
        to[384:608, :] = own_ref[0, BLK : BLK + 224]

    def block_of(n):
        return 2 * ((n // 2) ^ flip) + n % 2

    def scores(n, s_ref):
        local = block_of(n)
        j = half * 4 + local
        start = pl.multiple_of(local * BLK, BLK)
        q = q_ref[pl.ds(start, BLK), :]
        sn = dot_nt(q, kn[pl.ds(start, BLK), :])
        sn = sn + jnp.where((s == 0) & (j == 0), NEG, 0.0)
        s_ref[:, 0:256] = sn
        top = jnp.maximum(sn[:, :128], sn[:, 128:])
        rows = lax.broadcasted_iota(jnp.int32, (BLK, BLK), 0)
        cols = lax.broadcasted_iota(jnp.int32, (BLK, BLK), 1)
        sd = dot_nt(q, kn[pl.ds(start + BLK, BLK), :])
        sd = jnp.where(cols <= rows, sd, NEG)
        s_ref[:, 256:512] = sd
        top = jnp.maximum(top, jnp.maximum(sd[:, :128], sd[:, 128:]))
        col = lax.broadcasted_iota(jnp.int32, (1, 384), 1)
        ok = jnp.minimum(col - MIDB * (R1 - 8 * s - j), (R1 - 1) * MIDB - 1 - col) >= 0
        sm = dot_nt(q, km[pl.ds(pl.multiple_of(j * MIDB, MIDB), 384), :])
        sm = sm + jnp.where(ok, 0.0, NEG)
        s_ref[:, 512:896] = sm
        for i in range(3):
            top = jnp.maximum(top, sm[:, i * 128 : i * 128 + 128])
        for i in range(4):
            sf = dot_nt(q, far_refs[i][0, 0]) + far_ok_ref[pl.ds(j, 1), i * 256 : i * 256 + 256]
            s_ref[:, 896 + i * 256 : 1152 + i * 256] = sf
            top = jnp.maximum(top, jnp.maximum(sf[:, :128], sf[:, 128:]))
        return jnp.max(top, axis=1, keepdims=True)

    def finish(n, s_ref, top, o_ref):
        local = block_of(n)
        j = half * 4 + local
        start = pl.multiple_of(local * BLK, BLK)

        def weights(a, b):
            return jnp.exp2((s_ref[:, a:b] - top) * EXP_SCALE).astype(BF)

        acc = dot_ones(weights(0, 512), vn[pl.ds(start, 512), :], 1)
        mids = vm[pl.ds(pl.multiple_of(j * MIDB, MIDB), 384), :]
        acc = acc + dot_ones(weights(512, 896), mids, P1)
        for i in range(4):
            acc = acc + dot_ones(weights(896 + i * 256, 1152 + i * 256), far_refs[i][0, 1], P2)
        at = (n % 2) * BLK
        o_ref[at : at + BLK, :] = (acc[:, :HD] / acc[:, HD:]).astype(BF)

    slots = (sa, sb)
    top = scores(0, sa)
    for n in range(4):
        later = scores(n + 1, slots[(n + 1) % 2]) if n < 3 else None
        finish(n, slots[n % 2], top, (oa_ref, ob_ref)[n // 2])
        top = later


def attend(first, heads, info, queries, key_rows, value_rows, far_ok, own_k, own_v, back_k, back_v, back2, *fars):
    def rows(count, row):
        return pl.BlockSpec((count, HD), lambda h, info: (row(info), first + h))

    half = rows(1024, lambda info: info[1])
    before = rows(BLK, lambda info: 3 * info[1])
    head = lambda count: pl.BlockSpec((1, 2, count, HD), lambda h, info: (first + h, 0, 0, 0))
    out = pl.BlockSpec((512, HD), lambda h, info: (0, h))
    return pl.pallas_call(
        attend_kernel,
        grid_spec=pltpu.PrefetchScalarGridSpec(
            num_scalar_prefetch=1,
            grid=(heads,),
            in_specs=[half, half, half, before, before]
            + [pl.BlockSpec((8, FARS), lambda h, info: (0, 0))]
            + [pl.BlockSpec((1, 2 * BLK, HD), lambda h, info: (first + h, 0, 0))] * 4
            + [head(128)]
            + [head(256)] * 3
            + [pl.BlockSpec((1, 2, 256, HD), lambda h, info: (h, 0, 0, 0))],
            out_specs=[out, out],
            scratch_shapes=[
                pltpu.VMEM((1280, HD), BF),
                pltpu.VMEM((1280, HD), BF),
                pltpu.VMEM((MIDS, HD), BF),
                pltpu.VMEM((MIDS, HD), BF),
                pltpu.VMEM((BLK, KEYS), jnp.float32),
                pltpu.VMEM((BLK, KEYS), jnp.float32),
            ],
        ),
        out_shape=[jax.ShapeDtypeStruct((512, heads * HD), BF)] * 2,
        compiler_params=pltpu.CompilerParams(vmem_limit_bytes=VMEM_LIMIT),
        cost_estimate=pl.CostEstimate(
            flops=heads * 4 * BLK * KEYS * HD * 8,
            bytes_accessed=heads * HD * 2 * 6000,
            transcendentals=heads * 4 * BLK * KEYS,
        ),
        name="attend",
    )(info, queries, key_rows, value_rows, key_rows, value_rows, far_ok, own_k, own_v, back_k, back_v, back2, *fars)


def place_kernel(columns, me_ref, *refs):
    count = len(columns)
    pieces, out_ref, held, in_sems, out_sems = refs[:count], *refs[count:]
    me = me_ref[0]
    loads, stores = [], []
    for i in range(count):
        loads.append(pltpu.make_async_copy(pieces[i], held[i], in_sems.at[i]))
        loads[i].start()
    for i, (k, at) in enumerate(columns):
        to = pl.multiple_of((me ^ k) * 1024 + at, HD)
        width = pieces[i].shape[1]
        stores.append(
            pltpu.make_async_copy(held[i], out_ref.at[:, pl.ds(to, width)], out_sems.at[i])
        )
        loads[i].wait()
        stores[i].start()
    for store in stores:
        store.wait()


def place(me, pieces, columns):
    count = len(pieces)
    return pl.pallas_call(
        lambda *refs: place_kernel(columns, *refs),
        in_specs=[pl.BlockSpec(memory_space=pltpu.SMEM)]
        + [pl.BlockSpec(memory_space=pl.ANY)] * count,
        out_specs=pl.BlockSpec(memory_space=pl.ANY),
        out_shape=jax.ShapeDtypeStruct((512, 4096), BF),
        scratch_shapes=[
            [pltpu.VMEM(piece.shape, BF) for piece in pieces],
            pltpu.SemaphoreType.DMA((count,)),
            pltpu.SemaphoreType.DMA((count,)),
        ],
        compiler_params=pltpu.CompilerParams(vmem_limit_bytes=VMEM_LIMIT),
        cost_estimate=pl.CostEstimate(
            flops=0, bytes_accessed=count * 1024 * 1024, transcendentals=0
        ),
        name="place",
    )(me, *pieces)


def swap_heads(piece, k):
    return lax.ppermute(piece, "head", [(i, i ^ k) for i in range(4)])


def far_bias(s):
    x, z, y = s // 16, (s // 4) % 4, s % 4
    of = jnp.array(FROM, jnp.int32)
    zs = ((z + of) % 4).reshape(4, 1, 1, 1)
    ys = ((y + of) % 4).reshape(1, 4, 1, 1)
    xs = (x ^ jnp.arange(2, dtype=jnp.int32)).reshape(1, 1, 2, 1)
    group = (xs * 16 + zs * 4 + ys) * FARD + jnp.arange(FARD, dtype=jnp.int32)
    limit = (8 * s + jnp.arange(8, dtype=jnp.int32) - R1) * (BLK // P2)
    return jnp.where(group.reshape(1, FARS) < limit[:, None], 0.0, NEG)


def shards(queries, key_rows, value_rows):
    s = lax.axis_index("seq").astype(jnp.int32)
    me = lax.axis_index("head").astype(jnp.int32)
    pair, flip = me // 2, me % 2
    over = lambda value, route: lax.ppermute(value, "seq", route)
    firsts = [sum(CHUNKS[:c]) for c in range(len(CHUNKS))]
    own_k, own_v, last, f0 = pool(0, HEADS, key_rows, value_rows)
    g0 = jnp.concatenate([f0, over(f0, X_ROUTE)], axis=2)
    g0, own_v = lax.optimization_barrier((g0, own_v))
    above = over(own_v, UP_Z)
    g1, g3 = over(g0, Y_DOWN), over(g0, Y_UP)
    g1, g3, own_k, last = lax.optimization_barrier((g1, g3, own_k, last))
    back2 = over(last, shift_route(2))
    gs = [g0, g1, g3, over(g1, Y_DOWN)]
    own_v, gs, above, back2 = lax.optimization_barrier((own_v, gs, above, back2))
    back_k = over(own_k, shift_route(1))
    back_v = jnp.where(s % 4 == 0, over(above, ROUND_Y), over(own_v, ALONG_Y))
    h0 = jnp.concatenate(gs, axis=2)
    h1, h3 = over(h0, Z_DOWN), over(h0, Z_UP)
    h1, back_k = lax.optimization_barrier((h1, back_k))
    split = CHUNKS[0]
    h2 = (over(h1[:split], Z_DOWN), over(h3[split:], Z_UP))
    parts = (far_bias(s), own_k, own_v, back_k, back_v, back2, h0, h1, h3)
    pieces = {}
    args = (queries, key_rows, value_rows)
    for which, names in ((1 - pair, (2, 3)), (pair, (0, 1))):
        for c, (first, heads) in enumerate(zip(firsts, CHUNKS)):
            outs = attend(first, heads, jnp.stack([s, which, flip]), *args, *parts, h2[c])
            for k, out in zip(names, outs):
                if (c, k) == (1, 1):
                    out, pieces[1, 2], pieces[1, 3] = lax.optimization_barrier(
                        (out, pieces[1, 2], pieces[1, 3])
                    )
                pieces[c, k] = swap_heads(out, k) if k else out
            args = lax.optimization_barrier((*args, outs[0]))[:3]
    order = sorted(pieces, key=lambda at: (at[0], at[1]))
    return place(
        me.reshape(1), [pieces[at] for at in order], [(k, firsts[c] * HD) for c, k in order]
    )


def solution(mesh):
    return jax.shard_map(
        shards,
        mesh=mesh,
        in_specs=(P("seq", "head"), P("seq", "head"), P("seq", "head")),
        out_specs=P(("seq", "head"), None),
        check_vma=False,
    )
```

```python
import math

import jax
import jax.numpy as jnp
from jax import lax
from jax.experimental import pallas as pl
from jax.experimental.pallas import tpu as pltpu
from jax.sharding import PartitionSpec as P

HD = 128
BLK = 256
P1 = 8
P2 = 64
R1 = 12
SEQ = 32
TOK = 2048
HEADS = 8
NEG = -1e30
MIDB = BLK // P1
FARD = TOK // P2
FARS = SEQ * FARD
MIDS = 19 * MIDB
KEYS = 512 + 384 + FARS
EXP_SCALE = math.log2(math.e) / math.sqrt(HD)
CHUNKS = (4, 4)
VMEM_LIMIT = 56 * 1024 * 1024
BF = jnp.bfloat16


def seq_route(move):
    route = []
    for s in range(SEQ):
        x, z, y = move(s // 16, (s // 4) % 4, s % 4)
        route.append((s, x * 16 + (z % 4) * 4 + y % 4))
    return route


Y_UP = seq_route(lambda x, z, y: (x, z, y + 1))
Y_DOWN = seq_route(lambda x, z, y: (x, z, y - 1))
X_ROUTE = seq_route(lambda x, z, y: (1 - x, z, y))
Z_UP = seq_route(lambda x, z, y: (x, z + 1, y))
Z_DOWN = seq_route(lambda x, z, y: (x, z - 1, y))
FROM = (0, 1, 3, 2)


def shift_route(distance):
    return [(i - distance, i) for i in range(distance, SEQ)]


ALONG_Y = [(i, i + 1) for i in range(SEQ) if i % 4 < 3]
UP_Z = [(i, i + 4) for i in range(3, SEQ - 4, 4)]
ROUND_Y = [(i, i - 3) for i in range(7, SEQ, 4)]


def pool_kernel(k_ref, v_ref, send_k_ref, send_v_ref, mid2_ref, far_ref):
    rows = lax.broadcasted_iota(jnp.int32, (48, BLK), 0)
    cols = lax.broadcasted_iota(jnp.int32, (48, BLK), 1)
    mid = jnp.where(cols // P1 == rows, 1.0, 0.0)
    far = jnp.where(cols // P2 == rows - 32, 1.0, 0.0)
    heads = k_ref.shape[1] // HD
    for i, (ref, send_ref) in enumerate(((k_ref, send_k_ref), (v_ref, send_v_ref))):
        group = (mid / P1, far / P2) if i == 0 else (mid, far)
        take = jnp.where(rows < 32, group[0], group[1]).astype(BF)
        fars = []
        for b in range(TOK // BLK):
            pooled = jnp.dot(
                take, ref[b * BLK : (b + 1) * BLK, :], preferred_element_type=jnp.float32
            )
            mids = pooled[:32].astype(BF)
            for h in range(heads):
                piece = mids[:, h * HD : (h + 1) * HD]
                send_ref[h, BLK + b * MIDB : BLK + (b + 1) * MIDB, :] = piece
                if b >= 4:
                    mid2_ref[h, i, (b - 4) * MIDB : (b - 3) * MIDB, :] = piece
            fars.append(pooled[32:36])
        fars = jnp.concatenate(fars, axis=0).astype(BF)
        for h in range(heads):
            send_ref[h, :BLK, :] = ref[TOK - BLK :, h * HD : (h + 1) * HD]
            far_ref[h, i] = fars[:, h * HD : (h + 1) * HD]


def pool(first, heads, key_rows, value_rows):
    step = 2
    return pl.pallas_call(
        pool_kernel,
        grid=(heads // step,),
        in_specs=[pl.BlockSpec((TOK, step * HD), lambda i: (0, first // step + i))] * 2,
        out_specs=[
            pl.BlockSpec((step, 2 * BLK, HD), lambda i: (i, 0, 0)),
            pl.BlockSpec((step, 2 * BLK, HD), lambda i: (i, 0, 0)),
            pl.BlockSpec((step, 2, 128, HD), lambda i: (i, 0, 0, 0)),
            pl.BlockSpec((step, 2, FARD, HD), lambda i: (i, 0, 0, 0)),
        ],
        out_shape=[
            jax.ShapeDtypeStruct((heads, 2 * BLK, HD), BF),
            jax.ShapeDtypeStruct((heads, 2 * BLK, HD), BF),
            jax.ShapeDtypeStruct((heads, 2, 128, HD), BF),
            jax.ShapeDtypeStruct((heads, 2, FARD, HD), BF),
        ],
        compiler_params=pltpu.CompilerParams(vmem_limit_bytes=VMEM_LIMIT),
        cost_estimate=pl.CostEstimate(
            flops=2 * 2 * TOK * heads * HD * 48,
            bytes_accessed=2 * TOK * heads * HD * 3,
            transcendentals=0,
        ),
        name="pool",
    )(key_rows, value_rows)


def dot_nt(a, b):
    return lax.dot_general(a, b, (((1,), (1,)), ((), ())), preferred_element_type=jnp.float32)


def dot_ones(weights, values, one):
    wide = jnp.concatenate([values, jnp.full(values.shape, one, BF)], axis=1)
    return jnp.dot(weights, wide, preferred_element_type=jnp.float32)


def attend_kernel(
    info_ref, q_ref, k_ref, v_ref, kp_ref, vp_ref, far_ok_ref, own_k_ref, own_v_ref, back_k_ref, back_v_ref, back2_ref,
    h0_ref, h1_ref, h2_ref, h3_ref, oa_ref, ob_ref, kn, vn, km, vm, sa, sb,
):
    s = info_ref[0]
    half = info_ref[1]
    flip = info_ref[2]

    far_refs = (h0_ref, h1_ref, h2_ref, h3_ref)
    from_other = jnp.full((BLK, HD), half, jnp.int32) == 0
    kn[:BLK, :] = jnp.where(from_other, back_k_ref[0, :BLK], kp_ref[...])
    vn[:BLK, :] = jnp.where(from_other, back_v_ref[0, :BLK], vp_ref[...])
    kn[BLK:, :] = k_ref[...]
    vn[BLK:, :] = v_ref[...]
    for i, (to, back_ref, own_ref) in enumerate(
        ((km, back_k_ref, own_k_ref), (vm, back_v_ref, own_v_ref))
    ):
        to[0:128, :] = back2_ref[0, i]
        to[128:384, :] = back_ref[0, BLK:]
        to[384:608, :] = own_ref[0, BLK : BLK + 224]

    def block_of(n):
        return 2 * ((n // 2) ^ flip) + n % 2

    def scores(n, s_ref):
        local = block_of(n)
        j = half * 4 + local
        start = pl.multiple_of(local * BLK, BLK)
        q = q_ref[pl.ds(start, BLK), :]
        sn = dot_nt(q, kn[pl.ds(start, BLK), :])
        sn = sn + jnp.where((s == 0) & (j == 0), NEG, 0.0)
        s_ref[:, 0:256] = sn
        top = jnp.maximum(sn[:, :128], sn[:, 128:])
        rows = lax.broadcasted_iota(jnp.int32, (BLK, BLK), 0)
        cols = lax.broadcasted_iota(jnp.int32, (BLK, BLK), 1)
        sd = dot_nt(q, kn[pl.ds(start + BLK, BLK), :])
        sd = jnp.where(cols <= rows, sd, NEG)
        s_ref[:, 256:512] = sd
        top = jnp.maximum(top, jnp.maximum(sd[:, :128], sd[:, 128:]))
        col = lax.broadcasted_iota(jnp.int32, (1, 384), 1)
        ok = jnp.minimum(col - MIDB * (R1 - 8 * s - j), (R1 - 1) * MIDB - 1 - col) >= 0
        sm = dot_nt(q, km[pl.ds(pl.multiple_of(j * MIDB, MIDB), 384), :])
        sm = sm + jnp.where(ok, 0.0, NEG)
        s_ref[:, 512:896] = sm
        for i in range(3):
            top = jnp.maximum(top, sm[:, i * 128 : i * 128 + 128])
        for i in range(4):
            sf = dot_nt(q, far_refs[i][0, 0]) + far_ok_ref[pl.ds(j, 1), i * 256 : i * 256 + 256]
            s_ref[:, 896 + i * 256 : 1152 + i * 256] = sf
            top = jnp.maximum(top, jnp.maximum(sf[:, :128], sf[:, 128:]))
        return jnp.max(top, axis=1, keepdims=True)

    def finish(n, s_ref, top, o_ref):
        local = block_of(n)
        j = half * 4 + local
        start = pl.multiple_of(local * BLK, BLK)

        def weights(a, b):
            return jnp.exp2((s_ref[:, a:b] - top) * EXP_SCALE).astype(BF)

        acc = dot_ones(weights(0, 512), vn[pl.ds(start, 512), :], 1)
        mids = vm[pl.ds(pl.multiple_of(j * MIDB, MIDB), 384), :]
        acc = acc + dot_ones(weights(512, 896), mids, P1)
        for i in range(4):
            acc = acc + dot_ones(weights(896 + i * 256, 1152 + i * 256), far_refs[i][0, 1], P2)
        at = (n % 2) * BLK
        o_ref[at : at + BLK, :] = (acc[:, :HD] / acc[:, HD:]).astype(BF)

    slots = (sa, sb)
    top = scores(0, sa)
    for n in range(4):
        later = scores(n + 1, slots[(n + 1) % 2]) if n < 3 else None
        finish(n, slots[n % 2], top, (oa_ref, ob_ref)[n // 2])
        top = later


def attend(first, heads, info, queries, key_rows, value_rows, far_ok, own_k, own_v, back_k, back_v, back2, *fars):
    def rows(count, row):
        return pl.BlockSpec((count, HD), lambda h, info: (row(info), first + h))

    half = rows(1024, lambda info: info[1])
    before = rows(BLK, lambda info: 3 * info[1])
    head = lambda count: pl.BlockSpec((1, 2, count, HD), lambda h, info: (first + h, 0, 0, 0))
    out = pl.BlockSpec((512, HD), lambda h, info: (0, h))
    return pl.pallas_call(
        attend_kernel,
        grid_spec=pltpu.PrefetchScalarGridSpec(
            num_scalar_prefetch=1,
            grid=(heads,),
            in_specs=[half, half, half, before, before]
            + [pl.BlockSpec((8, FARS), lambda h, info: (0, 0))]
            + [pl.BlockSpec((1, 2 * BLK, HD), lambda h, info: (first + h, 0, 0))] * 4
            + [head(128)]
            + [head(256)] * 4,
            out_specs=[out, out],
            scratch_shapes=[
                pltpu.VMEM((1280, HD), BF),
                pltpu.VMEM((1280, HD), BF),
                pltpu.VMEM((MIDS, HD), BF),
                pltpu.VMEM((MIDS, HD), BF),
                pltpu.VMEM((BLK, KEYS), jnp.float32),
                pltpu.VMEM((BLK, KEYS), jnp.float32),
            ],
        ),
        out_shape=[jax.ShapeDtypeStruct((512, heads * HD), BF)] * 2,
        compiler_params=pltpu.CompilerParams(vmem_limit_bytes=VMEM_LIMIT),
        cost_estimate=pl.CostEstimate(
            flops=heads * 4 * BLK * KEYS * HD * 8,
            bytes_accessed=heads * HD * 2 * 6000,
            transcendentals=heads * 4 * BLK * KEYS,
        ),
        name="attend",
    )(info, queries, key_rows, value_rows, key_rows, value_rows, far_ok, own_k, own_v, back_k, back_v, back2, *fars)


def place_kernel(columns, me_ref, *refs):
    count = len(columns)
    pieces, out_ref, held, in_sems, out_sems = refs[:count], *refs[count:]
    me = me_ref[0]
    loads, stores = [], []
    for i in range(count):
        loads.append(pltpu.make_async_copy(pieces[i], held[i], in_sems.at[i]))
        loads[i].start()
    for i, (k, at) in enumerate(columns):
        to = pl.multiple_of((me ^ k) * 1024 + at, HD)
        width = pieces[i].shape[1]
        stores.append(
            pltpu.make_async_copy(held[i], out_ref.at[:, pl.ds(to, width)], out_sems.at[i])
        )
        loads[i].wait()
        stores[i].start()
    for store in stores:
        store.wait()


def place(me, pieces, columns):
    count = len(pieces)
    return pl.pallas_call(
        lambda *refs: place_kernel(columns, *refs),
        in_specs=[pl.BlockSpec(memory_space=pltpu.SMEM)]
        + [pl.BlockSpec(memory_space=pl.ANY)] * count,
        out_specs=pl.BlockSpec(memory_space=pl.ANY),
        out_shape=jax.ShapeDtypeStruct((512, 4096), BF),
        scratch_shapes=[
            [pltpu.VMEM(piece.shape, BF) for piece in pieces],
            pltpu.SemaphoreType.DMA((count,)),
            pltpu.SemaphoreType.DMA((count,)),
        ],
        compiler_params=pltpu.CompilerParams(vmem_limit_bytes=VMEM_LIMIT),
        cost_estimate=pl.CostEstimate(
            flops=0, bytes_accessed=count * 1024 * 1024, transcendentals=0
        ),
        name="place",
    )(me, *pieces)


def swap_heads(piece, k):
    return lax.ppermute(piece, "head", [(i, i ^ k) for i in range(4)])


def far_bias(s):
    x, z, y = s // 16, (s // 4) % 4, s % 4
    of = jnp.array(FROM, jnp.int32)
    zs = ((z + of) % 4).reshape(4, 1, 1, 1)
    ys = ((y + of) % 4).reshape(1, 4, 1, 1)
    xs = (x ^ jnp.arange(2, dtype=jnp.int32)).reshape(1, 1, 2, 1)
    group = (xs * 16 + zs * 4 + ys) * FARD + jnp.arange(FARD, dtype=jnp.int32)
    limit = (8 * s + jnp.arange(8, dtype=jnp.int32) - R1) * (BLK // P2)
    return jnp.where(group.reshape(1, FARS) < limit[:, None], 0.0, NEG)


def shards(queries, key_rows, value_rows):
    s = lax.axis_index("seq").astype(jnp.int32)
    me = lax.axis_index("head").astype(jnp.int32)
    pair, flip = me // 2, me % 2
    over = lambda value, route: lax.ppermute(value, "seq", route)
    firsts = [sum(CHUNKS[:c]) for c in range(len(CHUNKS))]
    own_k, own_v, last, f0 = pool(0, HEADS, key_rows, value_rows)
    g0 = jnp.concatenate([f0, over(f0, X_ROUTE)], axis=2)
    g0, own_v = lax.optimization_barrier((g0, own_v))
    above = over(own_v, UP_Z)
    g1, g3 = over(g0, Y_DOWN), over(g0, Y_UP)
    g1, g3, own_k, last = lax.optimization_barrier((g1, g3, own_k, last))
    back2 = over(last, shift_route(2))
    gs = [g0, g1, g3, over(g1, Y_DOWN)]
    own_v, gs, above, back2 = lax.optimization_barrier((own_v, gs, above, back2))
    back_k = over(own_k, shift_route(1))
    back_v = jnp.where(s % 4 == 0, over(above, ROUND_Y), over(own_v, ALONG_Y))
    h0 = jnp.concatenate(gs, axis=2)
    h1, h3 = over(h0, Z_DOWN), over(h0, Z_UP)
    h1, back_k = lax.optimization_barrier((h1, back_k))
    fars = [h0, h1, h3, over(h1, Z_DOWN)]
    parts = (far_bias(s), own_k, own_v, back_k, back_v, back2, *fars)
    pieces = {}
    args = (queries, key_rows, value_rows)
    calls = list(enumerate(zip(firsts, CHUNKS)))
    for which, names, these in ((1 - pair, (2, 3), calls), (pair, (0, 1), [(0, (0, HEADS))])):
        for c, (first, heads) in these:
            outs = attend(first, heads, jnp.stack([s, which, flip]), *args, *parts)
            for k, out in zip(names, outs):
                pieces[c, k] = swap_heads(out, k) if k else out
            args = lax.optimization_barrier((*args, outs[0]))[:3]
    order = sorted(pieces, key=lambda at: (at[0], at[1]))
    return place(
        me.reshape(1), [pieces[at] for at in order], [(k, firsts[c] * HD) for c, k in order]
    )


def solution(mesh):
    return jax.shard_map(
        shards,
        mesh=mesh,
        in_specs=(P("seq", "head"), P("seq", "head"), P("seq", "head")),
        out_specs=P(("seq", "head"), None),
        check_vma=False,
    )
```
